512 devices in a mesh: dp: 32 (over z, x), aug: 16 (over y, core).
Axes of the slice: x: 4, y: 8, z: 8, core: 2. Of those that a mesh axis runs over, the one named last changes fastest.
Arguments:
- images: bfloat16 [32, 3, 256, 256], P('dp'), may hold values from -8 to 8
- offsets: int32 [32, 16, 2], P('dp'), may hold values from 0 to 32
- flip_flags: int32 [32, 16], P('dp'), may hold values from 0 to 1
- out_grads: bfloat16 [32, 16, 256, 1664], P('dp', 'aug'), may hold values from -16 to 16
- weight: float32 [978432], P('aug'), may hold values from -3 to 3
- gauss_noise: float32 [978432], P('aug'), may hold values from -6 to 6
Outputs:
- new_weight: float32 [978432], P('aug')
- clipped_mean: float32 [978432], P('aug')
- grad_norms: float32 [32], P('dp')
The draws below stay inside these ranges and needn't reach their ends.
All inputs are finite; a program needn't handle non-finite values.
Results may differ from the reference program's by a relative error of at most 0.0003.
Values may be sent and summed in bfloat16 or wider, within the bound.
No kernel may reach another device: no remote copies, remote signals or barrier semaphores. Data moves between devices by JAX's collectives and lax.ppermute only.
A program may use at most 64 MiB of HBM per device.

```python
import math
import jax
import jax.numpy as jnp
from jax import lax

D = 1664
PS = 14
GRID = 16
CH = 3
PAD = 32
PATCH = 588
TOK = 256
SIDE = 256
IMAGES = 32
AUG = 16


def draw_images(key, part):
    key = jax.random.fold_in(key, 3)
    first, second = jax.random.split(key, 2)
    means = jax.random.normal(first, (IMAGES, CH, 1, 1), jnp.float32)
    rough = jax.random.normal(second, (IMAGES, CH, SIDE, SIDE), jnp.float32)
    return jnp.clip(means + rough, -8.0, 8.0).astype(jnp.bfloat16)


def draw_out_grads(key, part):
    key = jax.random.fold_in(key, 7)
    keys = jax.random.split(key, 5)
    sigma = math.sqrt(AUG / (TOK * 2.0))
    scales = jnp.exp(jax.random.uniform(keys[0], (IMAGES, 1, 1, 1), jnp.float32, math.log(0.05), math.log(5.0)))
    row_scale = jnp.exp(jax.random.uniform(keys[1], (IMAGES, AUG, TOK, 1), jnp.float32, 0.0, math.log(10.0))) / 4.64
    col_scale = jnp.exp(jax.random.uniform(keys[2], (1, 1, 1, D), jnp.float32, 0.0, math.log(10.0))) / 4.64
    common = jax.random.normal(keys[3], (IMAGES, 1, TOK, D), jnp.float32)
    own = jax.random.normal(keys[4], (IMAGES, AUG, TOK, D), jnp.float32)
    mixed = 0.6 * common + 0.8 * own
    values = sigma * scales * row_scale * col_scale * mixed
    return jnp.clip(values, -16.0, 16.0).astype(jnp.bfloat16)


def set_ends(array, own_key, smallest, largest):
    extent = array.shape
    index_at = [jax.random.randint(jax.random.fold_in(own_key, axis), (), 0, extent[axis]) for axis in range(len(extent))]
    array = array.at[tuple(index_at)].set(smallest)
    longest = extent.index(max(extent))
    index_at[longest] = (index_at[longest] + 1) % extent[longest]
    return array.at[tuple(index_at)].set(largest)


def block_levels(stream_key, shape, cuts, low, high):
    loudness = 1.0
    for position, blocks in cuts:
        steps = jax.random.uniform(jax.random.fold_in(jax.random.fold_in(stream_key, 6), position), (blocks,), jnp.float32, low / len(cuts), high / len(cuts))
        loudness = loudness * jnp.repeat(jnp.exp(steps), shape[position] // blocks).reshape((-1,) + (1,) * (len(shape) - 1 - position))
    return loudness


def gaussian(own_key, extent, scale, most, pieces=(), kind=jnp.bfloat16):
    gain = block_levels(own_key, extent, pieces, -0.22, 0.18) if pieces else 1.0
    entries = jax.random.normal(own_key, extent, jnp.float32) * scale * gain
    return jnp.minimum(jnp.maximum(entries, -most), most).astype(kind)


def setup_inputs(seed: int = 0) -> dict:
    arg_keys = jax.random.split(jax.random.key(seed), 7)
    return {
        "images": draw_images(jax.random.fold_in(arg_keys[6], 71), 0),
        "offsets": set_ends(jax.random.randint(arg_keys[1], (IMAGES, AUG, 2), 0, PAD + 1), jax.random.fold_in(arg_keys[1], 1), 0, PAD).astype(jnp.int32),
        "flip_flags": set_ends(jax.random.randint(arg_keys[2], (IMAGES, AUG), 0, 2), jax.random.fold_in(arg_keys[2], 1), 0, 1).astype(jnp.int32),
        "out_grads": draw_out_grads(jax.random.fold_in(arg_keys[6], 71), 0),
        "weight": gaussian(arg_keys[4], (PATCH * D,), 0.2, 3.0, ((0, 16),), jnp.float32),
        "gauss_noise": gaussian(arg_keys[5], (PATCH * D,), 1.0, 6.0, ((0, 16),), jnp.float32),
    }


def patches(picture, corner, flipped):
    anchor = jnp.zeros((), jnp.int32)
    cropped = lax.dynamic_slice(picture, (anchor, corner[0], corner[1]), (CH, GRID * PS, GRID * PS))
    cropped = jnp.where(flipped > 0, cropped[:, :, ::-1], cropped)
    blocks = cropped.reshape(CH, GRID, PS, GRID, PS).transpose(0, 2, 4, 1, 3)
    return blocks.reshape(CH * PS * PS, GRID * GRID)

def reference(images, offsets, flip_flags, out_grads, weight, gauss_noise):
    clip_bound = math.sqrt(PATCH * D)

    def one_image(running, inputs):
        picture, corners, flag_row, grad_rows = inputs
        patch_rows = jax.vmap(patches, in_axes=(None, 0, 0))(picture, corners, flag_row)
        summed = jnp.einsum('kpt,ktd->pd', patch_rows.astype(jnp.float32), grad_rows.astype(jnp.float32), precision=lax.Precision.HIGHEST)
        per_image = summed / AUG
        norm_value = jnp.sqrt(jnp.sum(per_image * per_image) + 1e-06)
        factor = jnp.minimum(1.0, clip_bound / norm_value)
        return (running + factor * per_image, norm_value)
    zero_sum = jnp.zeros((PATCH, D), jnp.float32)
    clipped_sum, grad_norms = lax.scan(one_image, zero_sum, (images, offsets, flip_flags, out_grads))
    clipped_sum = clipped_sum.reshape(PATCH * D)
    clipped_mean = clipped_sum / IMAGES
    new_weight = weight - 0.1 * (clipped_sum / clip_bound + gauss_noise)
    return (new_weight, clipped_mean, grad_norms)
```

```python
import functools
import math

import jax
import jax.numpy as jnp
from jax import lax
from jax.experimental import pallas as pl
from jax.experimental.pallas import tpu as pltpu
from jax.sharding import PartitionSpec as P

D = 1664
PS = 14
GRID = 16
CH = 3
SIDE = 256
PATCH = 588
AUG = 16
LANES = 128
BLOCKS = D // LANES
CLIP = math.sqrt(PATCH * D)
SHARD = PATCH * D // AUG
SROWS = 38
MROWS = 40
ROWS = 512
SPARE = 8
PITCH = SIDE + SPARE


def gradient_kernel(offs, flags, img, grads, msg, sel, cols, pat, gord, flat):
    lane = lax.broadcasted_iota(jnp.int32, (SIDE, SIDE), 1)
    row = lax.broadcasted_iota(jnp.int32, (SIDE, SIDE), 0)
    slot = lane // 16
    xpos = (lane % 16) * PS
    for k in range(AUG):
        pixel = xpos + ((slot + (16 - k)) % 16)
        corner = offs[k, 1]
        flipped = flags[k]
        first = jnp.where(flipped > 0, corner + (GRID * PS - 1), corner)
        sign = jnp.where(flipped > 0, -1, 1)
        hit = row == first + sign * pixel
        sel[:, k * SIDE:(k + 1) * SIDE] = jnp.where(hit, 1.0, 0.0).astype(jnp.bfloat16)

    for c in range(CH):
        for k in range(AUG):
            picked = jnp.dot(
                img[c], sel[:, k * SIDE:(k + 1) * SIDE], preferred_element_type=jnp.float32
            )
            for h in range(2):
                cols[c, 2 * k + h, 0:SIDE, :] = picked[:, h * LANES:(h + 1) * LANES]

    slots = lax.broadcasted_iota(jnp.int32, (8, LANES), 1) // 16
    masks = [slots == s for s in range(8)]

    def assemble(step, carry):
        c = step // GRID
        y = step % GRID
        for half in range(2):
            parts = []
            for k in range(AUG):
                start = offs[k, 0] + PS * y + 8 * half
                parts.append([cols[c, 2 * k + h, pl.ds(start, 8), :] for h in range(2)])
            for v in range(PS):
                pair = []
                for h in range(2):
                    value = None
                    for s in range(8):
                        k = (8 * h + s - v) % 16
                        piece = parts[k][h]
                        value = piece if value is None else jnp.where(masks[s], piece, value)
                    pair.append(value)
                shift = 16 * v
                turn = shift % LANES
                if turn:
                    low = pltpu.roll(pair[0], LANES - turn, 1)
                    high = pltpu.roll(pair[1], LANES - turn, 1)
                    keep = slots < (LANES - turn) // 16
                    pair = [jnp.where(keep, low, high), jnp.where(keep, high, low)]
                if shift >= LANES:
                    pair = pair[::-1]
                whole = jnp.concatenate(pair, axis=1)
                pat[half, v, c, :, pl.ds(pl.multiple_of(y * SIDE, SIDE), SIDE)] = whole
        return carry

    lax.fori_loop(0, CH * GRID, assemble, 0)

    for y in range(GRID):
        for k in range(AUG):
            gord[(y * AUG + k) * 16:(y * AUG + k + 1) * 16, :] = grads[k, y * 16:(y + 1) * 16, :]
    for half in range(2):
        taken = 8 if half == 0 else PS - 8
        for v in range(PS):
            left = pat[half, v].reshape(CH * 8, AUG * SIDE).astype(jnp.bfloat16)
            total = jnp.dot(left, gord[...], preferred_element_type=jnp.float32)
            for c in range(CH):
                first = c * PS * PS + half * 8 * PS + v
                flat[pl.ds(first, taken, stride=PS), :] = total[c * 8:c * 8 + taken, :]

    flat[PATCH:, :] = jnp.zeros((4, LANES), jnp.float32)
    values = flat[...]
    squares = jnp.sum(values * values)
    for b in range(AUG):
        first = 147 * b // 4
        msg[b, 0:SROWS, :] = flat[first:first + SROWS, :]
        msg[b, SROWS:MROWS, :] = jnp.full((MROWS - SROWS, LANES), squares, jnp.float32)


def shard_kernel(index, parts, term, norm, lined):
    squares = jnp.zeros((1, LANES), jnp.float32)
    for a in range(AUG):
        squares = squares + parts[a, SROWS:SROWS + 1, :]
    length = jnp.sqrt(squares / (AUG * AUG) + 1e-6)
    norm[...] = jnp.broadcast_to(length, (8, LANES))
    scale = jnp.minimum(1.0, CLIP / length) / AUG
    for a in range(BLOCKS):
        lined[pl.ds(a, SROWS, stride=BLOCKS), :] = parts[a, 0:SROWS, :] * scale
    lined[SROWS * BLOCKS:, :] = jnp.zeros((lined.shape[0] - SROWS * BLOCKS, LANES), jnp.float32)
    ahead = (index[0] * (SHARD % D)) % D
    rows = ahead // LANES
    lanes = ahead % LANES
    near = lined[pl.ds(rows, ROWS), :]
    far = lined[pl.ds(rows + 1, ROWS), :]
    lane = lax.broadcasted_iota(jnp.int32, (ROWS, LANES), 1)
    mixed = jnp.where(lane >= lanes, near, far)
    term[...] = pltpu.roll(mixed, (LANES - lanes) % LANES, 1)


VMEM = pl.BlockSpec(memory_space=pltpu.VMEM)
SMEM = pl.BlockSpec(memory_space=pltpu.SMEM)


def per_device(images, offsets, flip_flags, out_grads, weight, gauss_noise):
    aug_index = lax.axis_index("aug")
    images_in_all = lax.axis_size("dp")
    wide = jnp.pad(out_grads[0, 0], ((0, 0), (0, AUG * LANES - D)))
    blocks = wide.reshape(GRID * GRID, AUG, LANES).transpose(1, 0, 2)
    blocks = lax.all_to_all(blocks, "aug", 0, 0)
    parts = pl.pallas_call(
        gradient_kernel,
        out_shape=jax.ShapeDtypeStruct((AUG, MROWS, LANES), jnp.float32),
        in_specs=[SMEM, SMEM, VMEM, VMEM],
        out_specs=VMEM,
        scratch_shapes=[
            pltpu.VMEM((SIDE, AUG * SIDE), jnp.bfloat16),
            pltpu.VMEM((CH, 2 * AUG, PITCH, LANES), jnp.float32),
            pltpu.VMEM((2, PS, CH, 8, AUG * SIDE), jnp.float32),
            pltpu.VMEM((AUG * SIDE, LANES), jnp.bfloat16),
            pltpu.VMEM((PATCH + 4, LANES), jnp.float32),
        ],
        compiler_params=pltpu.CompilerParams(vmem_limit_bytes=52 * 1024 * 1024),
    )(offsets[0], flip_flags[0], images[0], blocks)
    parts = lax.all_to_all(parts, "aug", 0, 0)
    term, norm = pl.pallas_call(
        shard_kernel,
        out_shape=(
            jax.ShapeDtypeStruct((ROWS, LANES), jnp.float32),
            jax.ShapeDtypeStruct((8, LANES), jnp.float32),
        ),
        in_specs=[SMEM, VMEM],
        out_specs=(VMEM, VMEM),
        scratch_shapes=[pltpu.VMEM((ROWS + 16, LANES), jnp.float32)],
    )(aug_index.reshape(1), parts)
    pieces = lax.all_to_all(term.reshape(images_in_all, -1, LANES), "dp", 0, 0)
    piece = jnp.sum(pieces, axis=0)
    spread = jnp.broadcast_to(piece[None], pieces.shape)
    clipped_sum = lax.all_to_all(spread, "dp", 0, 0).reshape(-1)[:SHARD]
    clipped_mean = clipped_sum / images_in_all
    new_weight = weight - 0.1 * (clipped_sum / CLIP + gauss_noise)
    return (new_weight, clipped_mean, norm[0, 0:1])


def solution(mesh):
    return jax.shard_map(
        per_device,
        mesh=mesh,
        in_specs=(
            P("dp", None, None, None),
            P("dp", None, None),
            P("dp", None),
            P("dp", "aug", None, None),
            P("aug"),
            P("aug"),
        ),
        out_specs=(P("aug"), P("aug"), P("dp")),
        check_vma=False,
    )
```

```python
import functools
import math

import jax
import jax.numpy as jnp
from jax import lax
from jax.experimental import pallas as pl
from jax.experimental.pallas import tpu as pltpu
from jax.sharding import PartitionSpec as P

D = 1664
PS = 14
GRID = 16
CH = 3
SIDE = 256
PATCH = 588
AUG = 16
LANES = 128
BLOCKS = D // LANES
COLS = D // AUG
CLIP = math.sqrt(PATCH * D)
SHARD = PATCH * D // AUG
SROWS = 38
MROWS = 40
ROWS = 512
SPARE = 8
MIB = 1024 * 1024
PITCH = SIDE + SPARE


def patch_kernel(offs, flags, img, pat, sel, cols, held):
    lane = lax.broadcasted_iota(jnp.int32, (SIDE, SIDE), 1)
    row = lax.broadcasted_iota(jnp.int32, (SIDE, SIDE), 0)
    slot = lane // 16
    xpos = (lane % 16) * PS
    for k in range(AUG):
        pixel = xpos + ((slot + (16 - k)) % 16)
        corner = offs[k, 1]
        flipped = flags[k]
        first = jnp.where(flipped > 0, corner + (GRID * PS - 1), corner)
        sign = jnp.where(flipped > 0, -1, 1)
        hit = row == first + sign * pixel
        sel[:, k * SIDE:(k + 1) * SIDE] = jnp.where(hit, 1.0, 0.0).astype(jnp.bfloat16)

    for c in range(CH):
        for k in range(AUG):
            picked = jnp.dot(
                img[c], sel[:, k * SIDE:(k + 1) * SIDE], preferred_element_type=jnp.float32
            )
            for h in range(2):
                cols[c, 2 * k + h, 0:SIDE, :] = picked[:, h * LANES:(h + 1) * LANES]
            cols[c, 2 * k:2 * k + 2, SIDE:, :] = jnp.zeros((2, SPARE, LANES), jnp.float32)

    slots = lax.broadcasted_iota(jnp.int32, (8, LANES), 1) // 16
    masks = [slots == s for s in range(8)]

    def assemble(step, carry):
        c = step // GRID
        y = step % GRID
        for half in range(2):
            parts = []
            for k in range(AUG):
                start = offs[k, 0] + PS * y + 8 * half
                parts.append([cols[c, 2 * k + h, pl.ds(start, 8), :] for h in range(2)])
            for v in range(PS):
                pair = []
                for h in range(2):
                    value = None
                    for s in range(8):
                        k = (8 * h + s - v) % 16
                        piece = parts[k][h]
                        value = piece if value is None else jnp.where(masks[s], piece, value)
                    pair.append(value)
                shift = 16 * v
                turn = shift % LANES
                if turn:
                    low = pltpu.roll(pair[0], LANES - turn, 1)
                    high = pltpu.roll(pair[1], LANES - turn, 1)
                    keep = slots < (LANES - turn) // 16
                    pair = [jnp.where(keep, low, high), jnp.where(keep, high, low)]
                if shift >= LANES:
                    pair = pair[::-1]
                for h in range(2):
                    held[v, 8 * half:8 * half + 8, h * LANES:(h + 1) * LANES] = pair[h]
        for v in range(PS):
            place = pl.ds(pl.multiple_of(y * SIDE, SIDE), SIDE)
            pat[v, c, :, place] = held[v].astype(jnp.bfloat16)
        return carry

    lax.fori_loop(0, CH * GRID, assemble, 0)


def gradient_kernel(pat, grads, msg, near, gord, flat, sem):
    fetch = pltpu.make_async_copy(pat, near, sem)
    fetch.start()
    for k in range(AUG):
        turned = grads[k].T
        for y in range(GRID):
            gord[(y * AUG + k) * 16:(y * AUG + k + 1) * 16, :] = turned[y * 16:(y + 1) * 16, :]
    fetch.wait()
    left = near[...].reshape(PS * CH * 16, AUG * SIDE)
    total = jnp.dot(left, gord[...], preferred_element_type=jnp.float32)
    for v in range(PS):
        for c in range(CH):
            first = v * CH * 16 + c * 16
            flat[pl.ds(c * PS * PS + v, PS, stride=PS), 0:COLS] = total[first:first + PS, :]

    flat[PATCH:, 0:COLS] = jnp.zeros((4, COLS), jnp.float32)
    values = flat[:, 0:COLS]
    squares = jnp.sum(values * values)
    for b in range(AUG):
        first = 147 * b // 4
        msg[b, 0:SROWS, 0:COLS] = flat[first:first + SROWS, 0:COLS]
        msg[b, SROWS:MROWS, :] = jnp.full((MROWS - SROWS, LANES), squares, jnp.float32)


def shard_kernel(index, parts, term, norm, lined):
    squares = jnp.zeros((1, LANES), jnp.float32)
    for a in range(AUG):
        squares = squares + parts[a, SROWS:SROWS + 1, :]
    length = jnp.sqrt(squares / (AUG * AUG) + 1e-6)
    norm[...] = jnp.broadcast_to(length, (8, LANES))
    scale = jnp.minimum(1.0, CLIP / length) / AUG
    lane = lax.broadcasted_iota(jnp.int32, (SROWS, LANES), 1)
    for block in range(BLOCKS):
        value = None
        for a in range(LANES * block // COLS, (LANES * block + LANES - 1) // COLS + 1):
            begin = a * COLS - LANES * block
            piece = pltpu.roll(parts[a, 0:SROWS, :], begin % LANES, 1) * scale
            value = piece if value is None else jnp.where(lane >= begin, piece, value)
        lined[pl.ds(block, SROWS, stride=BLOCKS), :] = value
    lined[SROWS * BLOCKS:, :] = jnp.zeros((lined.shape[0] - SROWS * BLOCKS, LANES), jnp.float32)
    ahead = (index[0] * (SHARD % D)) % D
    rows = ahead // LANES
    lanes = ahead % LANES
    near = lined[pl.ds(rows, ROWS), :]
    far = lined[pl.ds(rows + 1, ROWS), :]
    lane = lax.broadcasted_iota(jnp.int32, (ROWS, LANES), 1)
    mixed = jnp.where(lane >= lanes, near, far)
    term[...] = pltpu.roll(mixed, (LANES - lanes) % LANES, 1)


VMEM = pl.BlockSpec(memory_space=pltpu.VMEM)
SMEM = pl.BlockSpec(memory_space=pltpu.SMEM)


def per_device(images, offsets, flip_flags, out_grads, weight, gauss_noise):
    aug_index = lax.axis_index("aug")
    images_in_all = lax.axis_size("dp")
    blocks = out_grads[0, 0].T.reshape(AUG, COLS, GRID * GRID)
    blocks = lax.all_to_all(blocks, "aug", 0, 0)
    pat = pl.pallas_call(
        patch_kernel,
        out_shape=jax.ShapeDtypeStruct((PS, CH, 16, AUG * SIDE), jnp.bfloat16),
        in_specs=[SMEM, SMEM, VMEM],
        out_specs=VMEM,
        scratch_shapes=[
            pltpu.VMEM((SIDE, AUG * SIDE), jnp.bfloat16),
            pltpu.VMEM((CH, 2 * AUG, PITCH, LANES), jnp.float32),
            pltpu.VMEM((PS, 16, SIDE), jnp.float32),
        ],
        compiler_params=pltpu.CompilerParams(vmem_limit_bytes=28 * MIB),
        cost_estimate=pl.CostEstimate(
            flops=20_000_000_000, bytes_accessed=20_000_000, transcendentals=0
        ),
    )(offsets[0], flip_flags[0], images[0])
    parts = pl.pallas_call(
        gradient_kernel,
        out_shape=jax.ShapeDtypeStruct((AUG, MROWS, LANES), jnp.float32),
        in_specs=[pl.BlockSpec(memory_space=pl.ANY), VMEM],
        out_specs=VMEM,
        scratch_shapes=[
            pltpu.VMEM((PS, CH, 16, AUG * SIDE), jnp.bfloat16),
            pltpu.VMEM((AUG * SIDE, COLS), jnp.bfloat16),
            pltpu.VMEM((PATCH + 4, LANES), jnp.float32),
            pltpu.SemaphoreType.DMA,
        ],
        compiler_params=pltpu.CompilerParams(vmem_limit_bytes=48 * MIB),
    )(pat, blocks)
    parts = lax.all_to_all(parts, "aug", 0, 0)
    term, norm = pl.pallas_call(
        shard_kernel,
        out_shape=(
            jax.ShapeDtypeStruct((ROWS, LANES), jnp.float32),
            jax.ShapeDtypeStruct((8, LANES), jnp.float32),
        ),
        in_specs=[SMEM, VMEM],
        out_specs=(VMEM, VMEM),
        scratch_shapes=[pltpu.VMEM((ROWS + 16, LANES), jnp.float32)],
        compiler_params=pltpu.CompilerParams(vmem_limit_bytes=8 * MIB),
    )(aug_index.reshape(1), parts)
    pieces = lax.all_to_all(term.reshape(images_in_all, -1, LANES), "dp", 0, 0)
    piece = jnp.sum(pieces, axis=0)
    spread = jnp.broadcast_to(piece[None], pieces.shape)
    clipped_sum = lax.all_to_all(spread, "dp", 0, 0).reshape(-1)[:SHARD]
    clipped_mean = clipped_sum / images_in_all
    new_weight = weight - 0.1 * (clipped_sum / CLIP + gauss_noise)
    return (new_weight, clipped_mean, norm[0, 0:1])


def solution(mesh):
    return jax.shard_map(
        per_device,
        mesh=mesh,
        in_specs=(
            P("dp", None, None, None),
            P("dp", None, None),
            P("dp", None),
            P("dp", "aug", None, None),
            P("aug"),
            P("aug"),
        ),
        out_specs=(P("aug"), P("aug"), P("dp")),
        check_vma=False,
    )
```

```python
import functools
import math

import jax
import jax.numpy as jnp
from jax import lax
from jax.experimental import pallas as pl
from jax.experimental.pallas import tpu as pltpu
from jax.sharding import PartitionSpec as P

D = 1664
PS = 14
GRID = 16
CH = 3
SIDE = 256
PATCH = 588
AUG = 16
LANES = 128
BLOCKS = D // LANES
COLS = D // AUG
CLIP = math.sqrt(PATCH * D)
SHARD = PATCH * D // AUG
SROWS = 38
MROWS = 48
PROWS = 15
ROWS = 480
FULL = 32700.0
LEVELS = 256.0
COARSE = 64.0
FINE = 1e6
SPARE = 8
MIB = 1024 * 1024
PITCH = SIDE + SPARE


def patch_kernel(offs, flags, img, pat, sel, cols, held):
    lane = lax.broadcasted_iota(jnp.int32, (SIDE, SIDE), 1)
    row = lax.broadcasted_iota(jnp.int32, (SIDE, SIDE), 0)
    slot = lane // 16
    xpos = (lane % 16) * PS
    for k in range(AUG):
        pixel = xpos + ((slot + (16 - k)) % 16)
        corner = offs[k, 1]
        flipped = flags[k]
        first = jnp.where(flipped > 0, corner + (GRID * PS - 1), corner)
        sign = jnp.where(flipped > 0, -1, 1)
        hit = row == first + sign * pixel
        sel[:, k * SIDE:(k + 1) * SIDE] = jnp.where(hit, 1.0, 0.0).astype(jnp.bfloat16)

    for c in range(CH):
        for k in range(AUG):
            picked = jnp.dot(
                img[c], sel[:, k * SIDE:(k + 1) * SIDE], preferred_element_type=jnp.float32
            )
            for h in range(2):
                cols[c, 2 * k + h, 0:SIDE, :] = picked[:, h * LANES:(h + 1) * LANES]
            cols[c, 2 * k:2 * k + 2, SIDE:, :] = jnp.zeros((2, SPARE, LANES), jnp.float32)

    slots = lax.broadcasted_iota(jnp.int32, (8, LANES), 1) // 16
    masks = [slots == s for s in range(8)]

    def assemble(step, carry):
        c = step // GRID
        y = step % GRID
        for half in range(2):
            parts = []
            for k in range(AUG):
                start = offs[k, 0] + PS * y + 8 * half
                parts.append([cols[c, 2 * k + h, pl.ds(start, 8), :] for h in range(2)])
            for v in range(PS):
                pair = []
                for h in range(2):
                    value = None
                    for s in range(8):
                        k = (8 * h + s - v) % 16
                        piece = parts[k][h]
                        value = piece if value is None else jnp.where(masks[s], piece, value)
                    pair.append(value)
                shift = 16 * v
                turn = shift % LANES
                if turn:
                    low = pltpu.roll(pair[0], LANES - turn, 1)
                    high = pltpu.roll(pair[1], LANES - turn, 1)
                    keep = slots < (LANES - turn) // 16
                    pair = [jnp.where(keep, low, high), jnp.where(keep, high, low)]
                if shift >= LANES:
                    pair = pair[::-1]
                for h in range(2):
                    held[v, 8 * half:8 * half + 8, h * LANES:(h + 1) * LANES] = pair[h]
        for v in range(PS):
            place = pl.ds(pl.multiple_of(y * SIDE, SIDE), SIDE)
            pat[v, c, :, place] = held[v].astype(jnp.bfloat16)
        return carry

    lax.fori_loop(0, CH * GRID, assemble, 0)


def gradient_kernel(pat, grads, msg, near, gord, flat, sem):
    fetch = pltpu.make_async_copy(pat, near, sem)
    fetch.start()
    flat[...] = jnp.zeros(flat.shape, jnp.float32)
    for k in range(AUG):
        turned = grads[k].T
        for y in range(GRID):
            gord[(y * AUG + k) * 16:(y * AUG + k + 1) * 16, :] = turned[y * 16:(y + 1) * 16, :]
    fetch.wait()
    left = near[...].reshape(PS * CH * 16, AUG * SIDE)
    total = jnp.dot(left, gord[...], preferred_element_type=jnp.float32)
    for v in range(PS):
        for c in range(CH):
            first = v * CH * 16 + c * 16
            flat[pl.ds(c * PS * PS + v, PS, stride=PS), 0:COLS] = total[first:first + PS, :]

    values = flat[:, 0:COLS]
    squares = jnp.full((1, LANES), jnp.sum(values * values), jnp.float32)
    coarse = jnp.floor(jnp.log(jnp.maximum(squares, 1e-36)) * COARSE)
    fine = (squares / jnp.exp(coarse / COARSE) - 1.0) * FINE
    row = lax.broadcasted_iota(jnp.int32, (MROWS, LANES), 0)
    inside = (row < SROWS) & (lax.broadcasted_iota(jnp.int32, (MROWS, LANES), 1) < COLS)
    tail = jnp.where(row == SROWS + 1, coarse, jnp.where(row == SROWS + 2, rounded(fine), 0.0))
    for b in range(AUG):
        first = 147 * b // 4
        block = jnp.where(inside, flat[first:first + MROWS, :], 0.0)
        codes, level = encode(block, jnp.abs(block))
        codes = jnp.where(row < SROWS, codes, jnp.where(row == SROWS, level, tail))
        msg[b] = codes.astype(jnp.int32).astype(jnp.int16)


def rounded(value):
    return jnp.clip(jnp.floor(value + 0.5), -32767.0, 32767.0)


def encode(block, sizes):
    most = jnp.max(sizes, axis=0, keepdims=True)
    level = jnp.ceil(jnp.log(jnp.maximum(most, 1e-30)) * LEVELS)
    return rounded(block * (FULL * jnp.exp(level * (-1.0 / LEVELS)))), level


def step_of(level):
    return jnp.exp(level * (1.0 / LEVELS)) * (1.0 / FULL)


def plain(codes):
    return codes.astype(jnp.int32).astype(jnp.float32)


def shard_kernel(index, parts, term, norm, lined, even):
    squares = jnp.zeros((1, LANES), jnp.float32)
    opened = []
    for a in range(AUG):
        part = plain(parts[a])
        opened.append(part[0:SROWS] * step_of(part[SROWS:SROWS + 1]))
        coarse, fine = part[SROWS + 1:SROWS + 2], part[SROWS + 2:SROWS + 3]
        squares = squares + jnp.exp(coarse / COARSE) * (1.0 + fine / FINE)
    length = jnp.sqrt(squares / (AUG * AUG) + 1e-6)
    norm[...] = jnp.broadcast_to(length, (8, LANES))
    scale = jnp.minimum(1.0, CLIP / length) / AUG
    lane = lax.broadcasted_iota(jnp.int32, (SROWS, LANES), 1)
    for block in range(BLOCKS):
        value = None
        for a in range(LANES * block // COLS, (LANES * block + LANES - 1) // COLS + 1):
            begin = a * COLS - LANES * block
            piece = pltpu.roll(opened[a], begin % LANES, 1) * scale
            value = piece if value is None else jnp.where(lane >= begin, piece, value)
        lined[pl.ds(block, SROWS, stride=BLOCKS), :] = value
    lined[SROWS * BLOCKS:, :] = jnp.zeros((lined.shape[0] - SROWS * BLOCKS, LANES), jnp.float32)
    ahead = (index[0] * (SHARD % D)) % D
    rows = ahead // LANES
    lanes = ahead % LANES
    near = lined[pl.ds(rows, ROWS), :]
    far = lined[pl.ds(rows + 1, ROWS), :]
    lane = lax.broadcasted_iota(jnp.int32, (ROWS, LANES), 1)
    mixed = jnp.where(lane >= lanes, near, far)
    even[0:ROWS, :] = pltpu.roll(mixed, (LANES - lanes) % LANES, 1)
    even[ROWS:, :] = jnp.zeros((8, LANES), jnp.float32)
    place = lax.broadcasted_iota(jnp.int32, (8, LANES), 0) * LANES + lax.broadcasted_iota(jnp.int32, (8, LANES), 1)
    inside = place < SHARD - (ROWS - 8) * LANES
    even[ROWS - 8:ROWS, :] = jnp.where(inside, even[ROWS - 8:ROWS, :], 0.0)
    for j in range(term.shape[0]):
        term[j] = coded_chunk(even[PROWS * j:PROWS * j + 16, :])


def coded_chunk(block):
    row = lax.broadcasted_iota(jnp.int32, (16, LANES), 0)
    codes, level = encode(block, jnp.where(row < PROWS, jnp.abs(block), 0.0))
    return jnp.where(row < PROWS, codes, level).astype(jnp.int32).astype(jnp.int16)


def total_kernel(pieces, spread):
    total = jnp.zeros((16, LANES), jnp.float32)
    for i in range(pieces.shape[0]):
        piece = plain(pieces[i])
        total = total + piece * step_of(piece[PROWS:PROWS + 1])
    codes = coded_chunk(total)
    for j in range(spread.shape[0]):
        spread[j] = codes


def open_kernel(chunks, shard):
    for j in range(chunks.shape[0]):
        chunk = plain(chunks[j])
        value = chunk * step_of(chunk[PROWS:PROWS + 1])
        shard[PROWS * j:PROWS * (j + 1), :] = value[0:PROWS]


VMEM = pl.BlockSpec(memory_space=pltpu.VMEM)
SMEM = pl.BlockSpec(memory_space=pltpu.SMEM)


def per_device(images, offsets, flip_flags, out_grads, weight, gauss_noise):
    aug_index = lax.axis_index("aug")
    images_in_all = lax.axis_size("dp")
    blocks = out_grads[0, 0].T.reshape(AUG, COLS, GRID * GRID)
    blocks = lax.all_to_all(blocks, "aug", 0, 0)
    pat = pl.pallas_call(
        patch_kernel,
        out_shape=jax.ShapeDtypeStruct((PS, CH, 16, AUG * SIDE), jnp.bfloat16),
        in_specs=[SMEM, SMEM, VMEM],
        out_specs=VMEM,
        scratch_shapes=[
            pltpu.VMEM((SIDE, AUG * SIDE), jnp.bfloat16),
            pltpu.VMEM((CH, 2 * AUG, PITCH, LANES), jnp.float32),
            pltpu.VMEM((PS, 16, SIDE), jnp.float32),
        ],
        compiler_params=pltpu.CompilerParams(vmem_limit_bytes=28 * MIB),
        cost_estimate=pl.CostEstimate(
            flops=20_000_000_000, bytes_accessed=20_000_000, transcendentals=0
        ),
    )(offsets[0], flip_flags[0], images[0])
    parts = pl.pallas_call(
        gradient_kernel,
        out_shape=jax.ShapeDtypeStruct((AUG, MROWS, LANES), jnp.int16),
        in_specs=[pl.BlockSpec(memory_space=pl.ANY), VMEM],
        out_specs=VMEM,
        scratch_shapes=[
            pltpu.VMEM((PS, CH, 16, AUG * SIDE), jnp.bfloat16),
            pltpu.VMEM((AUG * SIDE, COLS), jnp.bfloat16),
            pltpu.VMEM((PATCH + 12, LANES), jnp.float32),
            pltpu.SemaphoreType.DMA,
        ],
        compiler_params=pltpu.CompilerParams(vmem_limit_bytes=48 * MIB),
    )(pat, blocks)
    parts = lax.all_to_all(parts, "aug", 0, 0)
    chunks = jax.ShapeDtypeStruct((images_in_all, 16, LANES), jnp.int16)
    term, norm = pl.pallas_call(
        shard_kernel,
        out_shape=(chunks, jax.ShapeDtypeStruct((8, LANES), jnp.float32)),
        in_specs=[SMEM, VMEM],
        out_specs=(VMEM, VMEM),
        scratch_shapes=[
            pltpu.VMEM((ROWS + 32, LANES), jnp.float32),
            pltpu.VMEM((ROWS + 8, LANES), jnp.float32),
        ],
        compiler_params=pltpu.CompilerParams(vmem_limit_bytes=8 * MIB),
    )(aug_index.reshape(1), parts)
    pieces = lax.all_to_all(term, "dp", 0, 0)
    spread = pl.pallas_call(
        total_kernel,
        out_shape=chunks,
        in_specs=[VMEM],
        out_specs=VMEM,
        compiler_params=pltpu.CompilerParams(vmem_limit_bytes=8 * MIB),
    )(pieces)
    gathered = lax.all_to_all(spread, "dp", 0, 0)
    shard = pl.pallas_call(
        open_kernel,
        out_shape=jax.ShapeDtypeStruct((ROWS, LANES), jnp.float32),
        in_specs=[VMEM],
        out_specs=VMEM,
        compiler_params=pltpu.CompilerParams(vmem_limit_bytes=8 * MIB),
    )(gathered)
    clipped_sum = shard.reshape(-1)[:SHARD]
    clipped_mean = clipped_sum / images_in_all
    new_weight = weight - 0.1 * (clipped_sum / CLIP + gauss_noise)
    return (new_weight, clipped_mean, norm[0, 0:1])


def solution(mesh):
    return jax.shard_map(
        per_device,
        mesh=mesh,
        in_specs=(
            P("dp", None, None, None),
            P("dp", None, None),
            P("dp", None),
            P("dp", "aug", None, None),
            P("aug"),
            P("aug"),
        ),
        out_specs=(P("aug"), P("aug"), P("dp")),
        check_vma=False,
    )
```

```python
import functools
import math

import jax
import jax.numpy as jnp
from jax import lax
from jax.experimental import pallas as pl
from jax.experimental.pallas import tpu as pltpu
from jax.sharding import PartitionSpec as P

D = 1664
PS = 14
GRID = 16
CH = 3
SIDE = 256
PATCH = 588
AUG = 16
LANES = 128
BLOCKS = D // LANES
COLS = D // AUG
CLIP = math.sqrt(PATCH * D)
SHARD = PATCH * D // AUG
SROWS = 38
MROWS = 48
PROWS = 15
ROWS = 480
FULL = 32700.0
LEVELS = 256.0
COARSE = 64.0
FINE = 1e6
SPARE = 8
MIB = 1024 * 1024
EARLY = 7
ORDER = list(range(0, AUG, 2)) + list(range(1, AUG, 2))
PITCH = SIDE + SPARE


def patch_kernel(offs, flags, img, pat_early, pat_late, sel, cols):
    lane = lax.broadcasted_iota(jnp.int32, (SIDE, SIDE), 1)
    row = lax.broadcasted_iota(jnp.int32, (SIDE, SIDE), 0)
    slot = lane // 16
    xpos = (lane % 16) * PS
    for k in range(AUG):
        pixel = xpos + ((slot + (16 - k)) % 16)
        corner = offs[k, 1]
        flipped = flags[k]
        first = jnp.where(flipped > 0, corner + (GRID * PS - 1), corner)
        sign = jnp.where(flipped > 0, -1, 1)
        hit = row == first + sign * pixel
        sel[:, k * SIDE:(k + 1) * SIDE] = jnp.where(hit, 1.0, 0.0).astype(jnp.bfloat16)

    for c in range(CH):
        for k in range(AUG):
            picked = jnp.dot(
                img[c], sel[:, k * SIDE:(k + 1) * SIDE], preferred_element_type=jnp.float32
            )
            for h in range(2):
                cols[c, 2 * k + h, 0:SIDE, :] = picked[:, h * LANES:(h + 1) * LANES]
            cols[c, 2 * k:2 * k + 2, SIDE:, :] = jnp.zeros((2, SPARE, LANES), jnp.float32)

    slots = lax.broadcasted_iota(jnp.int32, (16, LANES), 1) // 16
    masks = [slots == s for s in range(8)]

    def assemble(pat, begin, count, step, carry):
        c = step // count
        place_y = step % count
        y = begin + place_y
        parts = []
        for k in range(AUG):
            rows = pl.ds(offs[k, 0] + PS * y, 16)
            parts.append([cols[c, 2 * k + h, rows, :].astype(jnp.bfloat16) for h in range(2)])
        for v in range(PS):
            pair = []
            for h in range(2):
                value = None
                for s in range(8):
                    piece = parts[(8 * h + s - v) % 16][h]
                    value = piece if value is None else jnp.where(masks[s], piece, value)
                pair.append(value)
            shift = 16 * v
            turn = shift % LANES
            if turn:
                low = pltpu.roll(pair[0], LANES - turn, 1)
                high = pltpu.roll(pair[1], LANES - turn, 1)
                keep = slots < (LANES - turn) // 16
                pair = [jnp.where(keep, low, high), jnp.where(keep, high, low)]
            if shift >= LANES:
                pair = pair[::-1]
            for h in range(2):
                place = pl.ds(pl.multiple_of(place_y * SIDE + h * LANES, LANES), LANES)
                pat[v, c, :, place] = pair[h]
        return carry

    for pat, begin, count in ((pat_early, 0, EARLY), (pat_late, EARLY, GRID - EARLY)):
        lax.fori_loop(0, CH * count, functools.partial(assemble, pat, begin, count), 0)


def gradient_kernel(pat_early, pat_late, grads, msg, near, gord, flat, sem):
    fetch = pltpu.make_async_copy(pat_late, near, sem)
    fetch.start()
    flat[...] = jnp.zeros(flat.shape, jnp.float32)
    for k in range(AUG):
        turned = grads[k].T
        for y in range(GRID):
            gord[(y * AUG + k) * 16:(y * AUG + k + 1) * 16, :] = turned[y * 16:(y + 1) * 16, :]
    total = jnp.dot(
        pat_early[...].reshape(PS * CH * 16, EARLY * SIDE),
        gord[0:EARLY * SIDE, :],
        preferred_element_type=jnp.float32,
    )
    fetch.wait()
    total = total + jnp.dot(
        near[...].reshape(PS * CH * 16, (GRID - EARLY) * SIDE),
        gord[EARLY * SIDE:, :],
        preferred_element_type=jnp.float32,
    )
    for v in range(PS):
        for c in range(CH):
            first = v * CH * 16 + c * 16
            flat[pl.ds(c * PS * PS + v, PS, stride=PS), 0:COLS] = total[first:first + PS, :]

    values = flat[:, 0:COLS]
    squares = jnp.full((1, LANES), jnp.sum(values * values), jnp.float32)
    coarse = jnp.floor(jnp.log(jnp.maximum(squares, 1e-36)) * COARSE)
    fine = (squares / jnp.exp(coarse / COARSE) - 1.0) * FINE
    row = lax.broadcasted_iota(jnp.int32, (MROWS, LANES), 0)
    inside = (row < SROWS) & (lax.broadcasted_iota(jnp.int32, (MROWS, LANES), 1) < COLS)
    tail = jnp.where(row == SROWS + 1, coarse, jnp.where(row == SROWS + 2, rounded(fine), 0.0))
    for order, b in enumerate(ORDER):
        first = 147 * b // 4
        block = jnp.where(inside, flat[first:first + MROWS, :], 0.0)
        codes, level = encode(block, jnp.abs(block))
        codes = jnp.where(row < SROWS, codes, jnp.where(row == SROWS, level, tail))
        msg[order] = codes.astype(jnp.int32).astype(jnp.int16)


def rounded(value):
    return jnp.clip(jnp.floor(value + 0.5), -32767.0, 32767.0)


def encode(block, sizes):
    most = jnp.max(sizes, axis=0, keepdims=True)
    level = jnp.ceil(jnp.log(jnp.maximum(most, 1e-30)) * LEVELS)
    return rounded(block * (FULL * jnp.exp(level * (-1.0 / LEVELS)))), level


def step_of(level):
    return jnp.exp(level * (1.0 / LEVELS)) * (1.0 / FULL)


def plain(codes):
    return codes.astype(jnp.int32).astype(jnp.float32)


def shard_kernel(index, parts, term, norm, lined, even):
    squares = jnp.zeros((1, LANES), jnp.float32)
    opened = []
    for a in range(AUG):
        part = plain(parts[ORDER.index(a)])
        opened.append(part[0:SROWS] * step_of(part[SROWS:SROWS + 1]))
        coarse, fine = part[SROWS + 1:SROWS + 2], part[SROWS + 2:SROWS + 3]
        squares = squares + jnp.exp(coarse / COARSE) * (1.0 + fine / FINE)
    length = jnp.sqrt(squares / (AUG * AUG) + 1e-6)
    norm[...] = jnp.broadcast_to(length, (8, LANES))
    scale = jnp.minimum(1.0, CLIP / length) / AUG
    lane = lax.broadcasted_iota(jnp.int32, (SROWS, LANES), 1)
    for block in range(BLOCKS):
        value = None
        for a in range(LANES * block // COLS, (LANES * block + LANES - 1) // COLS + 1):
            begin = a * COLS - LANES * block
            piece = pltpu.roll(opened[a], begin % LANES, 1) * scale
            value = piece if value is None else jnp.where(lane >= begin, piece, value)
        lined[pl.ds(block, SROWS, stride=BLOCKS), :] = value
    lined[SROWS * BLOCKS:, :] = jnp.zeros((lined.shape[0] - SROWS * BLOCKS, LANES), jnp.float32)
    ahead = (index[0] * (SHARD % D)) % D
    rows = ahead // LANES
    lanes = ahead % LANES
    near = lined[pl.ds(rows, ROWS), :]
    far = lined[pl.ds(rows + 1, ROWS), :]
    lane = lax.broadcasted_iota(jnp.int32, (ROWS, LANES), 1)
    mixed = jnp.where(lane >= lanes, near, far)
    even[0:ROWS, :] = pltpu.roll(mixed, (LANES - lanes) % LANES, 1)
    even[ROWS:, :] = jnp.zeros((8, LANES), jnp.float32)
    place = lax.broadcasted_iota(jnp.int32, (8, LANES), 0) * LANES + lax.broadcasted_iota(jnp.int32, (8, LANES), 1)
    inside = place < SHARD - (ROWS - 8) * LANES
    even[ROWS - 8:ROWS, :] = jnp.where(inside, even[ROWS - 8:ROWS, :], 0.0)
    for j in range(term.shape[0]):
        term[j] = coded_chunk(even[PROWS * j:PROWS * j + 16, :])


def coded_chunk(block):
    row = lax.broadcasted_iota(jnp.int32, (16, LANES), 0)
    codes, level = encode(block, jnp.where(row < PROWS, jnp.abs(block), 0.0))
    return jnp.where(row < PROWS, codes, level).astype(jnp.int32).astype(jnp.int16)


def total_kernel(pieces, spread):
    total = jnp.zeros((16, LANES), jnp.float32)
    for i in range(pieces.shape[0]):
        piece = plain(pieces[i])
        total = total + piece * step_of(piece[PROWS:PROWS + 1])
    codes = coded_chunk(total)
    for j in range(spread.shape[0]):
        spread[j] = codes


def open_kernel(chunks, shard):
    for j in range(chunks.shape[0]):
        chunk = plain(chunks[j])
        value = chunk * step_of(chunk[PROWS:PROWS + 1])
        shard[PROWS * j:PROWS * (j + 1), :] = value[0:PROWS]


VMEM = pl.BlockSpec(memory_space=pltpu.VMEM)
SMEM = pl.BlockSpec(memory_space=pltpu.SMEM)


def per_device(images, offsets, flip_flags, out_grads, weight, gauss_noise):
    aug_index = lax.axis_index("aug")
    images_in_all = lax.axis_size("dp")
    blocks = out_grads[0, 0].T.reshape(AUG, COLS, GRID * GRID)
    blocks = lax.all_to_all(blocks, "aug", 0, 0)
    pat_early, pat_late = pl.pallas_call(
        patch_kernel,
        out_shape=(
            jax.ShapeDtypeStruct((PS, CH, 16, EARLY * SIDE), jnp.bfloat16),
            jax.ShapeDtypeStruct((PS, CH, 16, (GRID - EARLY) * SIDE), jnp.bfloat16),
        ),
        in_specs=[SMEM, SMEM, VMEM],
        out_specs=(VMEM, VMEM),
        scratch_shapes=[
            pltpu.VMEM((SIDE, AUG * SIDE), jnp.bfloat16),
            pltpu.VMEM((CH, 2 * AUG, PITCH, LANES), jnp.float32),
        ],
        compiler_params=pltpu.CompilerParams(vmem_limit_bytes=20 * MIB),
        cost_estimate=pl.CostEstimate(
            flops=20_000_000_000, bytes_accessed=20_000_000, transcendentals=0
        ),
    )(offsets[0], flip_flags[0], images[0])
    parts = pl.pallas_call(
        gradient_kernel,
        out_shape=jax.ShapeDtypeStruct((AUG, MROWS, LANES), jnp.int16),
        in_specs=[VMEM, pl.BlockSpec(memory_space=pl.ANY), VMEM],
        out_specs=VMEM,
        scratch_shapes=[
            pltpu.VMEM((PS, CH, 16, (GRID - EARLY) * SIDE), jnp.bfloat16),
            pltpu.VMEM((AUG * SIDE, COLS), jnp.bfloat16),
            pltpu.VMEM((PATCH + 12, LANES), jnp.float32),
            pltpu.SemaphoreType.DMA,
        ],
        compiler_params=pltpu.CompilerParams(vmem_limit_bytes=48 * MIB),
    )(pat_early, pat_late, blocks)
    parts = lax.all_to_all(parts, "aug", 0, 0, axis_index_groups=[ORDER])
    chunks = jax.ShapeDtypeStruct((images_in_all, 16, LANES), jnp.int16)
    term, norm = pl.pallas_call(
        shard_kernel,
        out_shape=(chunks, jax.ShapeDtypeStruct((8, LANES), jnp.float32)),
        in_specs=[SMEM, VMEM],
        out_specs=(VMEM, VMEM),
        scratch_shapes=[
            pltpu.VMEM((ROWS + 32, LANES), jnp.float32),
            pltpu.VMEM((ROWS + 8, LANES), jnp.float32),
        ],
        compiler_params=pltpu.CompilerParams(vmem_limit_bytes=8 * MIB),
    )(aug_index.reshape(1), parts)
    pieces = lax.all_to_all(term, "dp", 0, 0)
    spread = pl.pallas_call(
        total_kernel,
        out_shape=chunks,
        in_specs=[VMEM],
        out_specs=VMEM,
        compiler_params=pltpu.CompilerParams(vmem_limit_bytes=8 * MIB),
    )(pieces)
    gathered = lax.all_to_all(spread, "dp", 0, 0)
    shard = pl.pallas_call(
        open_kernel,
        out_shape=jax.ShapeDtypeStruct((ROWS, LANES), jnp.float32),
        in_specs=[VMEM],
        out_specs=VMEM,
        compiler_params=pltpu.CompilerParams(vmem_limit_bytes=8 * MIB),
    )(gathered)
    clipped_sum = shard.reshape(-1)[:SHARD]
    clipped_mean = clipped_sum / images_in_all
    new_weight = weight - 0.1 * (clipped_sum / CLIP + gauss_noise)
    return (new_weight, clipped_mean, norm[0, 0:1])


def solution(mesh):
    return jax.shard_map(
        per_device,
        mesh=mesh,
        in_specs=(
            P("dp", None, None, None),
            P("dp", None, None),
            P("dp", None),
            P("dp", "aug", None, None),
            P("aug"),
            P("aug"),
        ),
        out_specs=(P("aug"), P("aug"), P("dp")),
        check_vma=False,
    )
```

```python
import functools
import math

import jax
import jax.numpy as jnp
from jax import lax
from jax.experimental import pallas as pl
from jax.experimental.pallas import tpu as pltpu
from jax.sharding import PartitionSpec as P

D = 1664
PS = 14
GRID = 16
CH = 3
SIDE = 256
PATCH = 588
AUG = 16
LANES = 128
BLOCKS = D // LANES
COLS = D // AUG
CLIP = math.sqrt(PATCH * D)
SHARD = PATCH * D // AUG
SROWS = 38
MROWS = 32
HELD = 40
PROWS = 15
ROWS = 480
FULL = 32700.0
LEVELS = 256.0
COARSE = 64.0
FINE = 1e6
SPARE = 8
MIB = 1024 * 1024
EARLY = 6
ORDER = list(range(0, AUG, 2)) + list(range(1, AUG, 2))
PITCH = SIDE + SPARE


def patch_kernel(offs, flags, img, pat_early, pat_late, sel, cols):
    lane = lax.broadcasted_iota(jnp.int32, (SIDE, SIDE), 1)
    row = lax.broadcasted_iota(jnp.int32, (SIDE, SIDE), 0)
    slot = lane // 16
    xpos = (lane % 16) * PS
    for k in range(AUG):
        pixel = xpos + ((slot + (16 - k)) % 16)
        corner = offs[k, 1]
        flipped = flags[k]
        first = jnp.where(flipped > 0, corner + (GRID * PS - 1), corner)
        sign = jnp.where(flipped > 0, -1, 1)
        hit = row == first + sign * pixel
        sel[:, k * SIDE:(k + 1) * SIDE] = jnp.where(hit, 1.0, 0.0).astype(jnp.bfloat16)

    for c in range(CH):
        for k in range(AUG):
            picked = jnp.dot(
                img[c], sel[:, k * SIDE:(k + 1) * SIDE], preferred_element_type=jnp.float32
            )
            for h in range(2):
                cols[c, 2 * k + h, 0:SIDE, :] = picked[:, h * LANES:(h + 1) * LANES]
            cols[c, 2 * k:2 * k + 2, SIDE:, :] = jnp.zeros((2, SPARE, LANES), jnp.float32)

    slots = lax.broadcasted_iota(jnp.int32, (16, LANES), 1) // 16
    masks = [slots == s for s in range(8)]

    def assemble(pat, begin, count, step, carry):
        c = step // count
        place_y = step % count
        y = begin + place_y
        parts = []
        for k in range(AUG):
            rows = pl.ds(offs[k, 0] + PS * y, 16)
            parts.append([cols[c, 2 * k + h, rows, :].astype(jnp.bfloat16) for h in range(2)])
        for v in range(PS):
            pair = []
            for h in range(2):
                value = None
                for s in range(8):
                    piece = parts[(8 * h + s - v) % 16][h]
                    value = piece if value is None else jnp.where(masks[s], piece, value)
                pair.append(value)
            shift = 16 * v
            turn = shift % LANES
            if turn:
                low = pltpu.roll(pair[0], LANES - turn, 1)
                high = pltpu.roll(pair[1], LANES - turn, 1)
                keep = slots < (LANES - turn) // 16
                pair = [jnp.where(keep, low, high), jnp.where(keep, high, low)]
            if shift >= LANES:
                pair = pair[::-1]
            for h in range(2):
                place = pl.ds(pl.multiple_of(place_y * SIDE + h * LANES, LANES), LANES)
                pat[v, c, :, place] = pair[h]
        return carry

    for pat, begin, count in ((pat_early, 0, EARLY), (pat_late, EARLY, GRID - EARLY)):
        lax.fori_loop(0, CH * count, functools.partial(assemble, pat, begin, count), 0)


def gradient_kernel(pat_early, pat_late, grads, msg, near, gord, flat, strip, sem):
    fetch = pltpu.make_async_copy(pat_late, near, sem)
    fetch.start()
    flat[...] = jnp.zeros(flat.shape, jnp.float32)
    for k in range(AUG):
        turned = grads[k].T
        for y in range(GRID):
            gord[(y * AUG + k) * 16:(y * AUG + k + 1) * 16, :] = turned[y * 16:(y + 1) * 16, :]
    total = jnp.dot(
        pat_early[...].reshape(PS * CH * 16, EARLY * SIDE),
        gord[0:EARLY * SIDE, :],
        preferred_element_type=jnp.float32,
    )
    fetch.wait()
    total = total + jnp.dot(
        near[...].reshape(PS * CH * 16, (GRID - EARLY) * SIDE),
        gord[EARLY * SIDE:, :],
        preferred_element_type=jnp.float32,
    )
    for v in range(PS):
        for c in range(CH):
            first = v * CH * 16 + c * 16
            flat[pl.ds(c * PS * PS + v, PS, stride=PS), 0:COLS] = total[first:first + PS, :]

    values = flat[:, 0:COLS]
    squares = jnp.full((1, LANES), jnp.sum(values * values), jnp.float32)
    coarse = jnp.floor(jnp.log(jnp.maximum(squares, 1e-36)) * COARSE)
    fine = (squares / jnp.exp(coarse / COARSE) - 1.0) * FINE
    row = lax.broadcasted_iota(jnp.int32, (HELD, LANES), 0)
    lane = lax.broadcasted_iota(jnp.int32, (HELD, LANES), 1)
    inside = (row < SROWS) & (lane < COLS)
    tail = jnp.where(lane < COLS, coarse, rounded(fine))
    for order, b in enumerate(ORDER):
        first = 147 * b // 4
        block = jnp.where(inside, flat[first:first + HELD, :], 0.0)
        codes, level = encode(block, jnp.abs(block))
        codes = jnp.where(row < SROWS, codes, jnp.where(row == SROWS, level, tail))
        over = codes[MROWS:]
        for q in range(4):
            strip[7 * q:7 * q + 8, :] = pltpu.roll(over, COLS - 24 * q, 1)
        upper, lower = pltpu.roll(over, 8, 1)[0:4], pltpu.roll(over, 16, 1)[4:8]
        strip[28:32, :] = jnp.where(lane[0:4] < COLS + 8, upper, lower)
        packed = jnp.where(lane[0:MROWS] < COLS, codes[0:MROWS], strip[...])
        msg[order] = packed.astype(jnp.int32).astype(jnp.int16)


def unpacked(part):
    row = lax.broadcasted_iota(jnp.int32, (8, LANES), 0)
    lane = lax.broadcasted_iota(jnp.int32, (8, LANES), 1)
    upper = pltpu.roll(pltpu.roll(part[24:32], LANES - 8, 1), 4, 0)
    over = jnp.where(row < 4, upper, pltpu.roll(part[24:32], LANES - 16, 1))
    for q in range(4):
        piece = pltpu.roll(part[7 * q:7 * q + 8], LANES - COLS + 24 * q, 1)
        over = jnp.where((lane >= 24 * q) & (lane < 24 * q + 24), piece, over)
    return over


def rounded(value):
    return jnp.clip(jnp.floor(value + 0.5), -32767.0, 32767.0)


def encode(block, sizes):
    most = jnp.max(sizes, axis=0, keepdims=True)
    level = jnp.ceil(jnp.log(jnp.maximum(most, 1e-30)) * LEVELS)
    return rounded(block * (FULL * jnp.exp(level * (-1.0 / LEVELS)))), level


def step_of(level):
    return jnp.exp(level * (1.0 / LEVELS)) * (1.0 / FULL)


def plain(codes):
    return codes.astype(jnp.int32).astype(jnp.float32)


def shard_kernel(index, parts, term, norm, lined, even):
    squares = jnp.zeros((1, 1), jnp.float32)
    opened = []
    for a in range(AUG):
        part = plain(parts[ORDER.index(a)])
        over = unpacked(part)
        step = step_of(over[6:7])
        opened.append(jnp.concatenate([part * step, over * step])[0:SROWS])
        coarse, fine = over[7:8, COLS - 8:COLS - 7], over[7:8, COLS:COLS + 1]
        squares = squares + jnp.exp(coarse / COARSE) * (1.0 + fine / FINE)
    length = jnp.sqrt(squares / (AUG * AUG) + 1e-6)
    norm[...] = jnp.broadcast_to(length, (8, LANES))
    scale = jnp.minimum(1.0, CLIP / length) / AUG
    lane = lax.broadcasted_iota(jnp.int32, (SROWS, LANES), 1)
    for block in range(BLOCKS):
        value = None
        for a in range(LANES * block // COLS, (LANES * block + LANES - 1) // COLS + 1):
            begin = a * COLS - LANES * block
            piece = pltpu.roll(opened[a], begin % LANES, 1) * scale
            value = piece if value is None else jnp.where(lane >= begin, piece, value)
        lined[pl.ds(block, SROWS, stride=BLOCKS), :] = value
    lined[SROWS * BLOCKS:, :] = jnp.zeros((lined.shape[0] - SROWS * BLOCKS, LANES), jnp.float32)
    ahead = (index[0] * (SHARD % D)) % D
    rows = ahead // LANES
    lanes = ahead % LANES
    near = lined[pl.ds(rows, ROWS), :]
    far = lined[pl.ds(rows + 1, ROWS), :]
    lane = lax.broadcasted_iota(jnp.int32, (ROWS, LANES), 1)
    mixed = jnp.where(lane >= lanes, near, far)
    even[0:ROWS, :] = pltpu.roll(mixed, (LANES - lanes) % LANES, 1)
    even[ROWS:, :] = jnp.zeros((8, LANES), jnp.float32)
    place = lax.broadcasted_iota(jnp.int32, (8, LANES), 0) * LANES + lax.broadcasted_iota(jnp.int32, (8, LANES), 1)
    inside = place < SHARD - (ROWS - 8) * LANES
    even[ROWS - 8:ROWS, :] = jnp.where(inside, even[ROWS - 8:ROWS, :], 0.0)
    for j in range(term.shape[0]):
        term[j] = coded_chunk(even[PROWS * j:PROWS * j + 16, :])


def coded_chunk(block):
    row = lax.broadcasted_iota(jnp.int32, (16, LANES), 0)
    codes, level = encode(block, jnp.where(row < PROWS, jnp.abs(block), 0.0))
    return jnp.where(row < PROWS, codes, level).astype(jnp.int32).astype(jnp.int16)


def total_kernel(pieces, spread):
    total = jnp.zeros((16, LANES), jnp.float32)
    for i in range(pieces.shape[0]):
        piece = plain(pieces[i])
        total = total + piece * step_of(piece[PROWS:PROWS + 1])
    codes = coded_chunk(total)
    for j in range(spread.shape[0]):
        spread[j] = codes


def open_kernel(chunks, shard):
    for j in range(chunks.shape[0]):
        chunk = plain(chunks[j])
        value = chunk * step_of(chunk[PROWS:PROWS + 1])
        shard[PROWS * j:PROWS * (j + 1), :] = value[0:PROWS]


VMEM = pl.BlockSpec(memory_space=pltpu.VMEM)
SMEM = pl.BlockSpec(memory_space=pltpu.SMEM)


def per_device(images, offsets, flip_flags, out_grads, weight, gauss_noise):
    aug_index = lax.axis_index("aug")
    images_in_all = lax.axis_size("dp")
    blocks = out_grads[0, 0].T.reshape(AUG, COLS, GRID * GRID)
    blocks = lax.all_to_all(blocks, "aug", 0, 0)
    pat_early, pat_late = pl.pallas_call(
        patch_kernel,
        out_shape=(
            jax.ShapeDtypeStruct((PS, CH, 16, EARLY * SIDE), jnp.bfloat16),
            jax.ShapeDtypeStruct((PS, CH, 16, (GRID - EARLY) * SIDE), jnp.bfloat16),
        ),
        in_specs=[SMEM, SMEM, VMEM],
        out_specs=(VMEM, VMEM),
        scratch_shapes=[
            pltpu.VMEM((SIDE, AUG * SIDE), jnp.bfloat16),
            pltpu.VMEM((CH, 2 * AUG, PITCH, LANES), jnp.float32),
        ],
        compiler_params=pltpu.CompilerParams(vmem_limit_bytes=20 * MIB),
        cost_estimate=pl.CostEstimate(
            flops=20_000_000_000, bytes_accessed=20_000_000, transcendentals=0
        ),
    )(offsets[0], flip_flags[0], images[0])
    parts = pl.pallas_call(
        gradient_kernel,
        out_shape=jax.ShapeDtypeStruct((AUG, MROWS, LANES), jnp.int16),
        in_specs=[VMEM, pl.BlockSpec(memory_space=pl.ANY), VMEM],
        out_specs=VMEM,
        scratch_shapes=[
            pltpu.VMEM((PS, CH, 16, (GRID - EARLY) * SIDE), jnp.bfloat16),
            pltpu.VMEM((AUG * SIDE, COLS), jnp.bfloat16),
            pltpu.VMEM((PATCH + 12, LANES), jnp.float32),
            pltpu.VMEM((MROWS, LANES), jnp.float32),
            pltpu.SemaphoreType.DMA,
        ],
        compiler_params=pltpu.CompilerParams(vmem_limit_bytes=48 * MIB),
    )(pat_early, pat_late, blocks)
    parts = lax.all_to_all(parts, "aug", 0, 0, axis_index_groups=[ORDER])
    chunks = jax.ShapeDtypeStruct((images_in_all, 16, LANES), jnp.int16)
    term, norm = pl.pallas_call(
        shard_kernel,
        out_shape=(chunks, jax.ShapeDtypeStruct((8, LANES), jnp.float32)),
        in_specs=[SMEM, VMEM],
        out_specs=(VMEM, VMEM),
        scratch_shapes=[
            pltpu.VMEM((ROWS + 32, LANES), jnp.float32),
            pltpu.VMEM((ROWS + 8, LANES), jnp.float32),
        ],
        compiler_params=pltpu.CompilerParams(vmem_limit_bytes=8 * MIB),
    )(aug_index.reshape(1), parts)
    pieces = lax.all_to_all(term, "dp", 0, 0)
    spread = pl.pallas_call(
        total_kernel,
        out_shape=chunks,
        in_specs=[VMEM],
        out_specs=VMEM,
        compiler_params=pltpu.CompilerParams(vmem_limit_bytes=8 * MIB),
    )(pieces)
    gathered = lax.all_to_all(spread, "dp", 0, 0)
    shard = pl.pallas_call(
        open_kernel,
        out_shape=jax.ShapeDtypeStruct((ROWS, LANES), jnp.float32),
        in_specs=[VMEM],
        out_specs=VMEM,
        compiler_params=pltpu.CompilerParams(vmem_limit_bytes=8 * MIB),
    )(gathered)
    clipped_sum = shard.reshape(-1)[:SHARD]
    clipped_mean = clipped_sum / images_in_all
    new_weight = weight - 0.1 * (clipped_sum / CLIP + gauss_noise)
    return (new_weight, clipped_mean, norm[0, 0:1])


def solution(mesh):
    return jax.shard_map(
        per_device,
        mesh=mesh,
        in_specs=(
            P("dp", None, None, None),
            P("dp", None, None),
            P("dp", None),
            P("dp", "aug", None, None),
            P("aug"),
            P("aug"),
        ),
        out_specs=(P("aug"), P("aug"), P("dp")),
        check_vma=False,
    )
```

```python
import functools
import math

import jax
import jax.numpy as jnp
from jax import lax
from jax.experimental import pallas as pl
from jax.experimental.pallas import tpu as pltpu
from jax.sharding import PartitionSpec as P

D = 1664
PS = 14
GRID = 16
CH = 3
SIDE = 256
PATCH = 588
AUG = 16
LANES = 128
BLOCKS = D // LANES
COLS = D // AUG
CLIP = math.sqrt(PATCH * D)
SHARD = PATCH * D // AUG
SROWS = 38
MROWS = 32
HELD = 40
PROWS = 15
ROWS = 480
FULL = 32700.0
LEVELS = 256.0
COARSE = 64.0
FINE = 1e6
SPARE = 8
MIB = 1024 * 1024
EARLY = 6
ORDER = list(range(0, AUG, 2)) + list(range(1, AUG, 2))
PITCH = SIDE + SPARE


def patch_kernel(offs, flags, img, pat_early, pat_late, sel, cols):
    lane = lax.broadcasted_iota(jnp.int32, (SIDE, SIDE), 1)
    row = lax.broadcasted_iota(jnp.int32, (SIDE, SIDE), 0)
    slot = lane // 16
    xpos = (lane % 16) * PS
    for k in range(AUG):
        pixel = xpos + ((slot + (16 - k)) % 16)
        corner = offs[k, 1]
        flipped = flags[k]
        first = jnp.where(flipped > 0, corner + (GRID * PS - 1), corner)
        sign = jnp.where(flipped > 0, -1, 1)
        hit = row == first + sign * pixel
        sel[:, k * SIDE:(k + 1) * SIDE] = jnp.where(hit, 1.0, 0.0).astype(jnp.bfloat16)

    for c in range(CH):
        for k in range(AUG):
            picked = jnp.dot(
                img[c], sel[:, k * SIDE:(k + 1) * SIDE], preferred_element_type=jnp.float32
            )
            for h in range(2):
                cols[c, 2 * k + h, 0:SIDE, :] = picked[:, h * LANES:(h + 1) * LANES]
            cols[c, 2 * k:2 * k + 2, SIDE:, :] = jnp.zeros((2, SPARE, LANES), jnp.float32)

    slots = lax.broadcasted_iota(jnp.int32, (16, LANES), 1) // 16
    masks = [slots == s for s in range(8)]

    def assemble(pat, begin, count, step, carry):
        c = step // count
        place_y = step % count
        y = begin + place_y
        parts = []
        for k in range(AUG):
            rows = pl.ds(offs[k, 0] + PS * y, 16)
            parts.append([cols[c, 2 * k + h, rows, :].astype(jnp.bfloat16) for h in range(2)])
        for v in range(PS):
            pair = []
            for h in range(2):
                value = None
                for s in range(8):
                    piece = parts[(8 * h + s - v) % 16][h]
                    value = piece if value is None else jnp.where(masks[s], piece, value)
                pair.append(value)
            shift = 16 * v
            turn = shift % LANES
            if turn:
                low = pltpu.roll(pair[0], LANES - turn, 1)
                high = pltpu.roll(pair[1], LANES - turn, 1)
                keep = slots < (LANES - turn) // 16
                pair = [jnp.where(keep, low, high), jnp.where(keep, high, low)]
            if shift >= LANES:
                pair = pair[::-1]
            for h in range(2):
                place = pl.ds(pl.multiple_of(place_y * SIDE + h * LANES, LANES), LANES)
                pat[v, c, :, place] = pair[h]
        return carry

    for pat, begin, count in ((pat_early, 0, EARLY), (pat_late, EARLY, GRID - EARLY)):
        lax.fori_loop(0, CH * count, functools.partial(assemble, pat, begin, count), 0)


def gradient_kernel(
    pat_early, pat_late, grads, msg, near, gord, flat, strip, total, sems
):
    late = near.shape[3] // 2
    fetches = []
    for half in range(2):
        part = pl.ds(half * late, late)
        fetches.append(
            pltpu.make_async_copy(
                pat_late.at[:, :, :, part], near.at[:, :, :, part], sems.at[half]
            )
        )
        fetches[half].start()

    def turn(k, carry):
        turned = grads[k].T
        for y in range(GRID):
            place = pl.ds(pl.multiple_of(y * AUG * 16 + k * 16, 16), 16)
            gord[place, :] = turned[y * 16:(y + 1) * 16, :]
        return carry

    def multiply(source, begin, end, first):
        def part(step, carry):
            many = PS // 2 * CH * 16
            left = source[pl.ds(step * (PS // 2), PS // 2), :, :, begin:end]
            value = jnp.dot(
                left.reshape(many, end - begin),
                gord[first:first + end - begin, :],
                preferred_element_type=jnp.float32,
            )
            rows = pl.ds(pl.multiple_of(step * many, 16), many)
            total[rows, :] = value if first == 0 else total[rows, :] + value
            return carry

        lax.fori_loop(0, 2, part, 0)

    flat[PATCH:, :] = jnp.zeros((12, LANES), jnp.float32)
    [turn(k, 0) for k in range(AUG)]
    multiply(pat_early, 0, EARLY * SIDE, 0)
    for half in range(2):
        fetches[half].wait()
        multiply(near, half * late, (half + 1) * late, EARLY * SIDE + half * late)
    for v in range(PS):
        for c in range(CH):
            first = v * CH * 16 + c * 16
            flat[pl.ds(c * PS * PS + v, PS, stride=PS), 0:COLS] = total[first:first + PS, :]

    values = flat[:, 0:COLS]
    squares = jnp.full((1, LANES), jnp.sum(values * values), jnp.float32)
    coarse = jnp.floor(jnp.log(jnp.maximum(squares, 1e-36)) * COARSE)
    fine = (squares / jnp.exp(coarse / COARSE) - 1.0) * FINE
    row = lax.broadcasted_iota(jnp.int32, (HELD, LANES), 0)
    lane = lax.broadcasted_iota(jnp.int32, (HELD, LANES), 1)
    inside = (row < SROWS) & (lane < COLS)
    tail = jnp.where(lane < COLS, coarse, rounded(fine))
    for order, b in enumerate(ORDER):
        first = 147 * b // 4
        block = jnp.where(inside, flat[first:first + HELD, :], 0.0)
        codes, level = encode(block, jnp.abs(block))
        codes = jnp.where(row < SROWS, codes, jnp.where(row == SROWS, level, tail))
        over = codes[MROWS:]
        for q in range(4):
            strip[7 * q:7 * q + 8, :] = pltpu.roll(over, COLS - 24 * q, 1)
        upper, lower = pltpu.roll(over, 8, 1)[0:4], pltpu.roll(over, 16, 1)[4:8]
        strip[28:32, :] = jnp.where(lane[0:4] < COLS + 8, upper, lower)
        packed = jnp.where(lane[0:MROWS] < COLS, codes[0:MROWS], strip[...])
        msg[order] = packed.astype(jnp.int32).astype(jnp.int16)


def unpacked(part):
    row = lax.broadcasted_iota(jnp.int32, (8, LANES), 0)
    lane = lax.broadcasted_iota(jnp.int32, (8, LANES), 1)
    upper = pltpu.roll(pltpu.roll(part[24:32], LANES - 8, 1), 4, 0)
    over = jnp.where(row < 4, upper, pltpu.roll(part[24:32], LANES - 16, 1))
    for q in range(4):
        piece = pltpu.roll(part[7 * q:7 * q + 8], LANES - COLS + 24 * q, 1)
        over = jnp.where((lane >= 24 * q) & (lane < 24 * q + 24), piece, over)
    return over


def rounded(value):
    return jnp.clip(jnp.floor(value + 0.5), -32767.0, 32767.0)


def encode(block, sizes):
    most = jnp.max(sizes, axis=0, keepdims=True)
    level = jnp.ceil(jnp.log(jnp.maximum(most, 1e-30)) * LEVELS)
    return rounded(block * (FULL * jnp.exp(level * (-1.0 / LEVELS)))), level


def step_of(level):
    return jnp.exp(level * (1.0 / LEVELS)) * (1.0 / FULL)


def plain(codes):
    return codes.astype(jnp.int32).astype(jnp.float32)


def shard_kernel(index, parts, term, norm, lined, even):
    squares = jnp.zeros((1, 1), jnp.float32)
    opened = []
    for a in range(AUG):
        part = plain(parts[ORDER.index(a)])
        over = unpacked(part)
        step = step_of(over[6:7])
        opened.append(jnp.concatenate([part * step, over * step])[0:SROWS])
        coarse, fine = over[7:8, COLS - 8:COLS - 7], over[7:8, COLS:COLS + 1]
        squares = squares + jnp.exp(coarse / COARSE) * (1.0 + fine / FINE)
    length = jnp.sqrt(squares / (AUG * AUG) + 1e-6)
    norm[...] = jnp.broadcast_to(length, (8, LANES))
    scale = jnp.minimum(1.0, CLIP / length) / AUG
    lane = lax.broadcasted_iota(jnp.int32, (SROWS, LANES), 1)
    for block in range(BLOCKS):
        value = None
        for a in range(LANES * block // COLS, (LANES * block + LANES - 1) // COLS + 1):
            begin = a * COLS - LANES * block
            piece = pltpu.roll(opened[a], begin % LANES, 1) * scale
            value = piece if value is None else jnp.where(lane >= begin, piece, value)
        lined[pl.ds(block, SROWS, stride=BLOCKS), :] = value
    lined[SROWS * BLOCKS:, :] = jnp.zeros((lined.shape[0] - SROWS * BLOCKS, LANES), jnp.float32)
    ahead = (index[0] * (SHARD % D)) % D
    rows = ahead // LANES
    lanes = ahead % LANES
    near = lined[pl.ds(rows, ROWS), :]
    far = lined[pl.ds(rows + 1, ROWS), :]
    lane = lax.broadcasted_iota(jnp.int32, (ROWS, LANES), 1)
    mixed = jnp.where(lane >= lanes, near, far)
    even[0:ROWS, :] = pltpu.roll(mixed, (LANES - lanes) % LANES, 1)
    even[ROWS:, :] = jnp.zeros((8, LANES), jnp.float32)
    place = lax.broadcasted_iota(jnp.int32, (8, LANES), 0) * LANES + lax.broadcasted_iota(jnp.int32, (8, LANES), 1)
    inside = place < SHARD - (ROWS - 8) * LANES
    even[ROWS - 8:ROWS, :] = jnp.where(inside, even[ROWS - 8:ROWS, :], 0.0)
    for j in range(term.shape[0]):
        term[j] = coded_chunk(even[PROWS * j:PROWS * j + 16, :])


def coded_chunk(block):
    row = lax.broadcasted_iota(jnp.int32, (16, LANES), 0)
    codes, level = encode(block, jnp.where(row < PROWS, jnp.abs(block), 0.0))
    return jnp.where(row < PROWS, codes, level).astype(jnp.int32).astype(jnp.int16)


def total_kernel(pieces, spread):
    total = jnp.zeros((16, LANES), jnp.float32)
    for i in range(pieces.shape[0]):
        piece = plain(pieces[i])
        total = total + piece * step_of(piece[PROWS:PROWS + 1])
    codes = coded_chunk(total)
    for j in range(spread.shape[0]):
        spread[j] = codes


def open_kernel(chunks, shard):
    for j in range(chunks.shape[0]):
        chunk = plain(chunks[j])
        value = chunk * step_of(chunk[PROWS:PROWS + 1])
        shard[PROWS * j:PROWS * (j + 1), :] = value[0:PROWS]


VMEM = pl.BlockSpec(memory_space=pltpu.VMEM)
SMEM = pl.BlockSpec(memory_space=pltpu.SMEM)


def per_device(images, offsets, flip_flags, out_grads, weight, gauss_noise):
    aug_index = lax.axis_index("aug")
    images_in_all = lax.axis_size("dp")
    blocks = out_grads[0, 0].T.reshape(AUG, COLS, GRID * GRID)
    blocks = lax.all_to_all(blocks, "aug", 0, 0)
    pat_early, pat_late = pl.pallas_call(
        patch_kernel,
        out_shape=(
            jax.ShapeDtypeStruct((PS, CH, 16, EARLY * SIDE), jnp.bfloat16),
            jax.ShapeDtypeStruct((PS, CH, 16, (GRID - EARLY) * SIDE), jnp.bfloat16),
        ),
        in_specs=[SMEM, SMEM, VMEM],
        out_specs=(VMEM, VMEM),
        scratch_shapes=[
            pltpu.VMEM((SIDE, AUG * SIDE), jnp.bfloat16),
            pltpu.VMEM((CH, 2 * AUG, PITCH, LANES), jnp.float32),
        ],
        compiler_params=pltpu.CompilerParams(vmem_limit_bytes=20 * MIB),
        cost_estimate=pl.CostEstimate(
            flops=20_000_000_000, bytes_accessed=20_000_000, transcendentals=0
        ),
    )(offsets[0], flip_flags[0], images[0])
    parts = pl.pallas_call(
        gradient_kernel,
        out_shape=jax.ShapeDtypeStruct((AUG, MROWS, LANES), jnp.int16),
        in_specs=[VMEM, pl.BlockSpec(memory_space=pl.ANY), VMEM],
        out_specs=VMEM,
        scratch_shapes=[
            pltpu.VMEM((PS, CH, 16, (GRID - EARLY) * SIDE), jnp.bfloat16),
            pltpu.VMEM((AUG * SIDE, COLS), jnp.bfloat16),
            pltpu.VMEM((PATCH + 12, LANES), jnp.float32),
            pltpu.VMEM((MROWS, LANES), jnp.float32),
            pltpu.VMEM((PS * CH * 16, COLS), jnp.float32),
            pltpu.SemaphoreType.DMA((2,)),
        ],
        compiler_params=pltpu.CompilerParams(vmem_limit_bytes=48 * MIB),
    )(pat_early, pat_late, blocks)
    parts = lax.all_to_all(parts, "aug", 0, 0, axis_index_groups=[ORDER])
    chunks = jax.ShapeDtypeStruct((images_in_all, 16, LANES), jnp.int16)
    term, norm = pl.pallas_call(
        shard_kernel,
        out_shape=(chunks, jax.ShapeDtypeStruct((8, LANES), jnp.float32)),
        in_specs=[SMEM, VMEM],
        out_specs=(VMEM, VMEM),
        scratch_shapes=[
            pltpu.VMEM((ROWS + 32, LANES), jnp.float32),
            pltpu.VMEM((ROWS + 8, LANES), jnp.float32),
        ],
        compiler_params=pltpu.CompilerParams(vmem_limit_bytes=8 * MIB),
    )(aug_index.reshape(1), parts)
    pieces = lax.all_to_all(term, "dp", 0, 0)
    spread = pl.pallas_call(
        total_kernel,
        out_shape=chunks,
        in_specs=[VMEM],
        out_specs=VMEM,
        compiler_params=pltpu.CompilerParams(vmem_limit_bytes=8 * MIB),
    )(pieces)
    gathered = lax.all_to_all(spread, "dp", 0, 0)
    shard = pl.pallas_call(
        open_kernel,
        out_shape=jax.ShapeDtypeStruct((ROWS, LANES), jnp.float32),
        in_specs=[VMEM],
        out_specs=VMEM,
        compiler_params=pltpu.CompilerParams(vmem_limit_bytes=8 * MIB),
    )(gathered)
    clipped_sum = shard.reshape(-1)[:SHARD]
    clipped_mean = clipped_sum / images_in_all
    new_weight = weight - 0.1 * (clipped_sum / CLIP + gauss_noise)
    return (new_weight, clipped_mean, norm[0, 0:1])


def solution(mesh):
    return jax.shard_map(
        per_device,
        mesh=mesh,
        in_specs=(
            P("dp", None, None, None),
            P("dp", None, None),
            P("dp", None),
            P("dp", "aug", None, None),
            P("aug"),
            P("aug"),
        ),
        out_specs=(P("aug"), P("aug"), P("dp")),
        check_vma=False,
    )
```

```python
import functools
import math

import jax
import jax.numpy as jnp
from jax import lax
from jax.experimental import pallas as pl
from jax.experimental.pallas import tpu as pltpu
from jax.sharding import PartitionSpec as P

D = 1664
PS = 14
GRID = 16
CH = 3
SIDE = 256
PATCH = 588
AUG = 16
LANES = 128
BLOCKS = D // LANES
COLS = D // AUG
CLIP = math.sqrt(PATCH * D)
SHARD = PATCH * D // AUG
SROWS = 38
MROWS = 32
HELD = 40
PROWS = 15
ROWS = 480
FULL = 32700.0
LEVELS = 256.0
COARSE = 64.0
FINE = 1e6
SPARE = 8
MIB = 1024 * 1024
EARLY = 6
LATE = (GRID - EARLY) // 2
ORDER = list(range(0, AUG, 2)) + list(range(1, AUG, 2))
PITCH = SIDE + SPARE


def patch_kernel(offs, flags, img, pat_early, pat_late, sel, cols):
    lane = lax.broadcasted_iota(jnp.int32, (SIDE, SIDE), 1)
    row = lax.broadcasted_iota(jnp.int32, (SIDE, SIDE), 0)
    slot = lane // 16
    xpos = (lane % 16) * PS
    for k in range(AUG):
        pixel = xpos + ((slot + (16 - k)) % 16)
        corner = offs[k, 1]
        flipped = flags[k]
        first = jnp.where(flipped > 0, corner + (GRID * PS - 1), corner)
        sign = jnp.where(flipped > 0, -1, 1)
        hit = row == first + sign * pixel
        sel[:, k * SIDE:(k + 1) * SIDE] = jnp.where(hit, 1.0, 0.0).astype(jnp.bfloat16)

    for c in range(CH):
        for k in range(AUG):
            picked = jnp.dot(
                img[c], sel[:, k * SIDE:(k + 1) * SIDE], preferred_element_type=jnp.float32
            )
            for h in range(2):
                cols[c, 2 * k + h, 0:SIDE, :] = picked[:, h * LANES:(h + 1) * LANES]
            cols[c, 2 * k:2 * k + 2, SIDE:, :] = jnp.zeros((2, SPARE, LANES), jnp.float32)

    slots = lax.broadcasted_iota(jnp.int32, (16, LANES), 1) // 16
    masks = [slots == s for s in range(8)]

    def assemble(pat, begin, count, step, carry):
        c = step // count
        place_y = step % count
        y = begin + place_y
        parts = []
        for k in range(AUG):
            rows = pl.ds(offs[k, 0] + PS * y, 16)
            parts.append([cols[c, 2 * k + h, rows, :].astype(jnp.bfloat16) for h in range(2)])
        for v in range(PS):
            pair = []
            for h in range(2):
                value = None
                for s in range(8):
                    piece = parts[(8 * h + s - v) % 16][h]
                    value = piece if value is None else jnp.where(masks[s], piece, value)
                pair.append(value)
            shift = 16 * v
            turn = shift % LANES
            if turn:
                low = pltpu.roll(pair[0], LANES - turn, 1)
                high = pltpu.roll(pair[1], LANES - turn, 1)
                keep = slots < (LANES - turn) // 16
                pair = [jnp.where(keep, low, high), jnp.where(keep, high, low)]
            if shift >= LANES:
                pair = pair[::-1]
            for h in range(2):
                place = pl.ds(pl.multiple_of(place_y * SIDE + h * LANES, LANES), LANES)
                pat[v, c, :, place] = pair[h]
        return carry

    pieces = [(pat_early, 0, EARLY)]
    pieces += [(pat_late.at[part], EARLY + part * LATE, LATE) for part in range(2)]
    for pat, begin, count in pieces:
        lax.fori_loop(0, CH * count, functools.partial(assemble, pat, begin, count), 0)


def gradient_kernel(
    pat_early, pat_late, grads, msg, near, gord, flat, strip, total, sems
):
    late = LATE * SIDE
    for part in range(2):
        pltpu.make_async_copy(pat_late.at[part], near.at[part], sems.at[part]).start()

    def turn(k):
        turned = grads[k].T
        for y in range(GRID):
            place = pl.ds(pl.multiple_of(y * AUG * 16 + k * 16, 16), 16)
            gord[place, :] = turned[y * 16:(y + 1) * 16, :]

    flat[PATCH:, :] = jnp.zeros((12, LANES), jnp.float32)
    for k in range(AUG):
        turn(k)
    total[:, 0:COLS] = jnp.dot(
        pat_early[...].reshape(PS * CH * 16, EARLY * SIDE),
        gord[0:EARLY * SIDE, :],
        preferred_element_type=jnp.float32,
    )

    def add_part(part, carry):
        pltpu.make_async_copy(pat_late.at[part], near.at[part], sems.at[part]).wait()
        rows = pl.ds(pl.multiple_of(EARLY * SIDE + part * late, 16), late)
        total[:, 0:COLS] = total[:, 0:COLS] + jnp.dot(
            near[part].reshape(PS * CH * 16, late),
            gord[rows, :],
            preferred_element_type=jnp.float32,
        )
        return carry

    lax.fori_loop(0, 2, add_part, 0)
    for v in range(PS):
        for c in range(CH):
            first = v * CH * 16 + c * 16
            flat[pl.ds(c * PS * PS + v, PS, stride=PS), 0:COLS] = total[first:first + PS, 0:COLS]

    values = flat[:, 0:COLS]
    squares = jnp.full((1, LANES), jnp.sum(values * values), jnp.float32)
    coarse = jnp.floor(jnp.log(jnp.maximum(squares, 1e-36)) * COARSE)
    fine = (squares / jnp.exp(coarse / COARSE) - 1.0) * FINE
    row = lax.broadcasted_iota(jnp.int32, (HELD, LANES), 0)
    lane = lax.broadcasted_iota(jnp.int32, (HELD, LANES), 1)
    inside = (row < SROWS) & (lane < COLS)
    tail = jnp.where(lane < COLS, coarse, rounded(fine))
    for order, b in enumerate(ORDER):
        first = 147 * b // 4
        block = jnp.where(inside, flat[first:first + HELD, :], 0.0)
        codes, level = encode(block, jnp.abs(block))
        codes = jnp.where(row < SROWS, codes, jnp.where(row == SROWS, level, tail))
        over = codes[MROWS:]
        for q in range(4):
            strip[7 * q:7 * q + 8, :] = pltpu.roll(over, COLS - 24 * q, 1)
        upper, lower = pltpu.roll(over, 8, 1)[0:4], pltpu.roll(over, 16, 1)[4:8]
        strip[28:32, :] = jnp.where(lane[0:4] < COLS + 8, upper, lower)
        packed = jnp.where(lane[0:MROWS] < COLS, codes[0:MROWS], strip[...])
        msg[order] = packed.astype(jnp.int32).astype(jnp.int16)


def unpacked(part):
    row = lax.broadcasted_iota(jnp.int32, (8, LANES), 0)
    lane = lax.broadcasted_iota(jnp.int32, (8, LANES), 1)
    upper = pltpu.roll(pltpu.roll(part[24:32], LANES - 8, 1), 4, 0)
    over = jnp.where(row < 4, upper, pltpu.roll(part[24:32], LANES - 16, 1))
    for q in range(4):
        piece = pltpu.roll(part[7 * q:7 * q + 8], LANES - COLS + 24 * q, 1)
        over = jnp.where((lane >= 24 * q) & (lane < 24 * q + 24), piece, over)
    return over


def rounded(value):
    return jnp.clip(jnp.floor(value + 0.5), -32767.0, 32767.0)


def encode(block, sizes):
    most = jnp.max(sizes, axis=0, keepdims=True)
    level = jnp.ceil(jnp.log(jnp.maximum(most, 1e-30)) * LEVELS)
    return rounded(block * (FULL * jnp.exp(level * (-1.0 / LEVELS)))), level


def step_of(level):
    return jnp.exp(level * (1.0 / LEVELS)) * (1.0 / FULL)


def plain(codes):
    return codes.astype(jnp.int32).astype(jnp.float32)


def shard_kernel(index, parts, term, norm, lined, even):
    squares = jnp.zeros((1, 1), jnp.float32)
    opened = []
    for a in range(AUG):
        part = plain(parts[ORDER.index(a)])
        over = unpacked(part)
        step = step_of(over[6:7])
        opened.append(jnp.concatenate([part * step, over * step])[0:SROWS])
        coarse, fine = over[7:8, COLS - 8:COLS - 7], over[7:8, COLS:COLS + 1]
        squares = squares + jnp.exp(coarse / COARSE) * (1.0 + fine / FINE)
    length = jnp.sqrt(squares / (AUG * AUG) + 1e-6)
    norm[...] = jnp.broadcast_to(length, (8, LANES))
    scale = jnp.minimum(1.0, CLIP / length) / AUG
    lane = lax.broadcasted_iota(jnp.int32, (SROWS, LANES), 1)
    for block in range(BLOCKS):
        value = None
        for a in range(LANES * block // COLS, (LANES * block + LANES - 1) // COLS + 1):
            begin = a * COLS - LANES * block
            piece = pltpu.roll(opened[a], begin % LANES, 1) * scale
            value = piece if value is None else jnp.where(lane >= begin, piece, value)
        lined[pl.ds(block, SROWS, stride=BLOCKS), :] = value
    lined[SROWS * BLOCKS:, :] = jnp.zeros((lined.shape[0] - SROWS * BLOCKS, LANES), jnp.float32)
    ahead = (index[0] * (SHARD % D)) % D
    rows = ahead // LANES
    lanes = ahead % LANES
    near = lined[pl.ds(rows, ROWS), :]
    far = lined[pl.ds(rows + 1, ROWS), :]
    lane = lax.broadcasted_iota(jnp.int32, (ROWS, LANES), 1)
    mixed = jnp.where(lane >= lanes, near, far)
    even[0:ROWS, :] = pltpu.roll(mixed, (LANES - lanes) % LANES, 1)
    even[ROWS:, :] = jnp.zeros((8, LANES), jnp.float32)
    place = lax.broadcasted_iota(jnp.int32, (8, LANES), 0) * LANES + lax.broadcasted_iota(jnp.int32, (8, LANES), 1)
    inside = place < SHARD - (ROWS - 8) * LANES
    even[ROWS - 8:ROWS, :] = jnp.where(inside, even[ROWS - 8:ROWS, :], 0.0)
    for j in range(term.shape[0]):
        term[j] = coded_chunk(even[PROWS * j:PROWS * j + 16, :])


def coded_chunk(block):
    row = lax.broadcasted_iota(jnp.int32, (16, LANES), 0)
    codes, level = encode(block, jnp.where(row < PROWS, jnp.abs(block), 0.0))
    return jnp.where(row < PROWS, codes, level).astype(jnp.int32).astype(jnp.int16)


def total_kernel(pieces, spread):
    total = jnp.zeros((16, LANES), jnp.float32)
    for i in range(pieces.shape[0]):
        piece = plain(pieces[i])
        total = total + piece * step_of(piece[PROWS:PROWS + 1])
    codes = coded_chunk(total)
    for j in range(spread.shape[0]):
        spread[j] = codes


def open_kernel(chunks, shard):
    for j in range(chunks.shape[0]):
        chunk = plain(chunks[j])
        value = chunk * step_of(chunk[PROWS:PROWS + 1])
        shard[PROWS * j:PROWS * (j + 1), :] = value[0:PROWS]


VMEM = pl.BlockSpec(memory_space=pltpu.VMEM)
SMEM = pl.BlockSpec(memory_space=pltpu.SMEM)


def per_device(images, offsets, flip_flags, out_grads, weight, gauss_noise):
    aug_index = lax.axis_index("aug")
    images_in_all = lax.axis_size("dp")
    blocks = out_grads[0, 0].T.reshape(AUG, COLS, GRID * GRID)
    blocks = lax.all_to_all(blocks, "aug", 0, 0)
    pat_early, pat_late = pl.pallas_call(
        patch_kernel,
        out_shape=(
            jax.ShapeDtypeStruct((PS, CH, 16, EARLY * SIDE), jnp.bfloat16),
            jax.ShapeDtypeStruct((2, PS, CH, 16, LATE * SIDE), jnp.bfloat16),
        ),
        in_specs=[SMEM, SMEM, VMEM],
        out_specs=(VMEM, VMEM),
        scratch_shapes=[
            pltpu.VMEM((SIDE, AUG * SIDE), jnp.bfloat16),
            pltpu.VMEM((CH, 2 * AUG, PITCH, LANES), jnp.float32),
        ],
        compiler_params=pltpu.CompilerParams(vmem_limit_bytes=20 * MIB),
        cost_estimate=pl.CostEstimate(
            flops=20_000_000_000, bytes_accessed=20_000_000, transcendentals=0
        ),
    )(offsets[0], flip_flags[0], images[0])
    parts = pl.pallas_call(
        gradient_kernel,
        out_shape=jax.ShapeDtypeStruct((AUG, MROWS, LANES), jnp.int16),
        in_specs=[VMEM, pl.BlockSpec(memory_space=pl.ANY), VMEM],
        out_specs=VMEM,
        scratch_shapes=[
            pltpu.VMEM((2, PS, CH, 16, LATE * SIDE), jnp.bfloat16),
            pltpu.VMEM((AUG * SIDE, COLS), jnp.bfloat16),
            pltpu.VMEM((PATCH + 12, LANES), jnp.float32),
            pltpu.VMEM((MROWS, LANES), jnp.float32),
            pltpu.VMEM((PS * CH * 16, LANES), jnp.float32),
            pltpu.SemaphoreType.DMA((2,)),
        ],
        compiler_params=pltpu.CompilerParams(vmem_limit_bytes=48 * MIB),
    )(pat_early, pat_late, blocks)
    parts = lax.all_to_all(parts, "aug", 0, 0, axis_index_groups=[ORDER])
    chunks = jax.ShapeDtypeStruct((images_in_all, 16, LANES), jnp.int16)
    term, norm = pl.pallas_call(
        shard_kernel,
        out_shape=(chunks, jax.ShapeDtypeStruct((8, LANES), jnp.float32)),
        in_specs=[SMEM, VMEM],
        out_specs=(VMEM, VMEM),
        scratch_shapes=[
            pltpu.VMEM((ROWS + 32, LANES), jnp.float32),
            pltpu.VMEM((ROWS + 8, LANES), jnp.float32),
        ],
        compiler_params=pltpu.CompilerParams(vmem_limit_bytes=8 * MIB),
    )(aug_index.reshape(1), parts)
    pieces = lax.all_to_all(term, "dp", 0, 0)
    spread = pl.pallas_call(
        total_kernel,
        out_shape=chunks,
        in_specs=[VMEM],
        out_specs=VMEM,
        compiler_params=pltpu.CompilerParams(vmem_limit_bytes=8 * MIB),
    )(pieces)
    gathered = lax.all_to_all(spread, "dp", 0, 0)
    shard = pl.pallas_call(
        open_kernel,
        out_shape=jax.ShapeDtypeStruct((ROWS, LANES), jnp.float32),
        in_specs=[VMEM],
        out_specs=VMEM,
        compiler_params=pltpu.CompilerParams(vmem_limit_bytes=8 * MIB),
    )(gathered)
    clipped_sum = shard.reshape(-1)[:SHARD]
    clipped_mean = clipped_sum / images_in_all
    new_weight = weight - 0.1 * (clipped_sum / CLIP + gauss_noise)
    return (new_weight, clipped_mean, norm[0, 0:1])


def solution(mesh):
    return jax.shard_map(
        per_device,
        mesh=mesh,
        in_specs=(
            P("dp", None, None, None),
            P("dp", None, None),
            P("dp", None),
            P("dp", "aug", None, None),
            P("aug"),
            P("aug"),
        ),
        out_specs=(P("aug"), P("aug"), P("dp")),
        check_vma=False,
    )
```

```python
import functools
import math

import jax
import jax.numpy as jnp
from jax import lax
from jax.experimental import pallas as pl
from jax.experimental.pallas import tpu as pltpu
from jax.sharding import PartitionSpec as P

D = 1664
PS = 14
GRID = 16
CH = 3
SIDE = 256
PATCH = 588
AUG = 16
LANES = 128
BLOCKS = D // LANES
COLS = D // AUG
CLIP = math.sqrt(PATCH * D)
SHARD = PATCH * D // AUG
SROWS = 38
MROWS = 32
HELD = 40
PROWS = 15
ROWS = 480
FULL = 32700.0
LEVELS = 256.0
COARSE = 64.0
FINE = 1e6
SPARE = 8
MIB = 1024 * 1024
EARLY = 6
LATE = (GRID - EARLY) // 2
ORDER = list(range(0, AUG, 2)) + list(range(1, AUG, 2))
PITCH = SIDE + SPARE


def patch_kernel(offs, flags, img, pat_early, pat_late, sel, cols):
    lane = lax.broadcasted_iota(jnp.int32, (SIDE, SIDE), 1)
    row = lax.broadcasted_iota(jnp.int32, (SIDE, SIDE), 0)
    slot = lane // 16
    xpos = (lane % 16) * PS
    for k in range(AUG):
        pixel = xpos + ((slot + (16 - k)) % 16)
        corner = offs[k, 1]
        flipped = flags[k]
        first = jnp.where(flipped > 0, corner + (GRID * PS - 1), corner)
        sign = jnp.where(flipped > 0, -1, 1)
        hit = row == first + sign * pixel
        sel[:, k * SIDE:(k + 1) * SIDE] = jnp.where(hit, 1.0, 0.0).astype(jnp.bfloat16)

    for c in range(CH):
        for k in range(AUG):
            picked = jnp.dot(
                img[c], sel[:, k * SIDE:(k + 1) * SIDE], preferred_element_type=jnp.float32
            )
            for h in range(2):
                cols[c, 2 * k + h, 0:SIDE, :] = picked[:, h * LANES:(h + 1) * LANES]
            cols[c, 2 * k:2 * k + 2, SIDE:, :] = jnp.zeros((2, SPARE, LANES), jnp.float32)

    slots = lax.broadcasted_iota(jnp.int32, (16, LANES), 1) // 16
    masks = [slots == s for s in range(8)]

    def assemble(pat, begin, count, step, carry):
        c = step // count
        place_y = step % count
        y = begin + place_y
        parts = []
        for k in range(AUG):
            rows = pl.ds(offs[k, 0] + PS * y, 16)
            parts.append([cols[c, 2 * k + h, rows, :].astype(jnp.bfloat16) for h in range(2)])
        for v in range(PS):
            pair = []
            for h in range(2):
                value = None
                for s in range(8):
                    piece = parts[(8 * h + s - v) % 16][h]
                    value = piece if value is None else jnp.where(masks[s], piece, value)
                pair.append(value)
            shift = 16 * v
            turn = shift % LANES
            if turn:
                low = pltpu.roll(pair[0], LANES - turn, 1)
                high = pltpu.roll(pair[1], LANES - turn, 1)
                keep = slots < (LANES - turn) // 16
                pair = [jnp.where(keep, low, high), jnp.where(keep, high, low)]
            if shift >= LANES:
                pair = pair[::-1]
            for h in range(2):
                place = pl.ds(pl.multiple_of(place_y * SIDE + h * LANES, LANES), LANES)
                pat[v, c, :, place] = pair[h]
        return carry

    pieces = [(pat_early, 0, EARLY)]
    pieces += [(pat_late.at[part], EARLY + part * LATE, LATE) for part in range(2)]
    for pat, begin, count in pieces:
        lax.fori_loop(0, CH * count, functools.partial(assemble, pat, begin, count), 0)


def gradient_kernel(
    pat_early, pat_late, grads, msg, near, gord, flat, strip, total, sems
):
    late = LATE * SIDE
    for part in range(2):
        pltpu.make_async_copy(pat_late.at[part], near.at[part], sems.at[part]).start()

    def turn(k):
        turned = grads[ORDER.index(k)].T
        for y in range(GRID):
            place = pl.ds(pl.multiple_of(y * AUG * 16 + k * 16, 16), 16)
            gord[place, :] = turned[y * 16:(y + 1) * 16, :]

    flat[PATCH:, :] = jnp.zeros((12, LANES), jnp.float32)
    for k in range(AUG):
        turn(k)
    total[:, 0:COLS] = jnp.dot(
        pat_early[...].reshape(PS * CH * 16, EARLY * SIDE),
        gord[0:EARLY * SIDE, :],
        preferred_element_type=jnp.float32,
    )

    def add_part(part, carry):
        pltpu.make_async_copy(pat_late.at[part], near.at[part], sems.at[part]).wait()
        rows = pl.ds(pl.multiple_of(EARLY * SIDE + part * late, 16), late)
        total[:, 0:COLS] = total[:, 0:COLS] + jnp.dot(
            near[part].reshape(PS * CH * 16, late),
            gord[rows, :],
            preferred_element_type=jnp.float32,
        )
        return carry

    lax.fori_loop(0, 2, add_part, 0)
    for v in range(PS):
        for c in range(CH):
            first = v * CH * 16 + c * 16
            flat[pl.ds(c * PS * PS + v, PS, stride=PS), 0:COLS] = total[first:first + PS, 0:COLS]

    values = flat[:, 0:COLS]
    squares = jnp.full((1, LANES), jnp.sum(values * values), jnp.float32)
    coarse = jnp.floor(jnp.log(jnp.maximum(squares, 1e-36)) * COARSE)
    fine = (squares / jnp.exp(coarse / COARSE) - 1.0) * FINE
    row = lax.broadcasted_iota(jnp.int32, (HELD, LANES), 0)
    lane = lax.broadcasted_iota(jnp.int32, (HELD, LANES), 1)
    inside = (row < SROWS) & (lane < COLS)
    tail = jnp.where(lane < COLS, coarse, rounded(fine))
    for order, b in enumerate(ORDER):
        first = 147 * b // 4
        block = jnp.where(inside, flat[first:first + HELD, :], 0.0)
        codes, level = encode(block, jnp.abs(block))
        codes = jnp.where(row < SROWS, codes, jnp.where(row == SROWS, level, tail))
        over = codes[MROWS:]
        for q in range(4):
            strip[7 * q:7 * q + 8, :] = pltpu.roll(over, COLS - 24 * q, 1)
        upper, lower = pltpu.roll(over, 8, 1)[0:4], pltpu.roll(over, 16, 1)[4:8]
        strip[28:32, :] = jnp.where(lane[0:4] < COLS + 8, upper, lower)
        packed = jnp.where(lane[0:MROWS] < COLS, codes[0:MROWS], strip[...])
        msg[order] = packed.astype(jnp.int32).astype(jnp.int16)


def unpacked(part):
    row = lax.broadcasted_iota(jnp.int32, (8, LANES), 0)
    lane = lax.broadcasted_iota(jnp.int32, (8, LANES), 1)
    upper = pltpu.roll(pltpu.roll(part[24:32], LANES - 8, 1), 4, 0)
    over = jnp.where(row < 4, upper, pltpu.roll(part[24:32], LANES - 16, 1))
    for q in range(4):
        piece = pltpu.roll(part[7 * q:7 * q + 8], LANES - COLS + 24 * q, 1)
        over = jnp.where((lane >= 24 * q) & (lane < 24 * q + 24), piece, over)
    return over


def rounded(value):
    return jnp.clip(jnp.floor(value + 0.5), -32767.0, 32767.0)


def encode(block, sizes):
    most = jnp.max(sizes, axis=0, keepdims=True)
    level = jnp.ceil(jnp.log(jnp.maximum(most, 1e-30)) * LEVELS)
    return rounded(block * (FULL * jnp.exp(level * (-1.0 / LEVELS)))), level


def step_of(level):
    return jnp.exp(level * (1.0 / LEVELS)) * (1.0 / FULL)


def plain(codes):
    return codes.astype(jnp.int32).astype(jnp.float32)


def shard_kernel(index, parts, term, norm, lined, even):
    squares = jnp.zeros((1, 1), jnp.float32)
    opened = []
    for a in range(AUG):
        part = plain(parts[a])
        over = unpacked(part)
        step = step_of(over[6:7])
        opened.append(jnp.concatenate([part * step, over * step])[0:SROWS])
        coarse, fine = over[7:8, COLS - 8:COLS - 7], over[7:8, COLS:COLS + 1]
        squares = squares + jnp.exp(coarse / COARSE) * (1.0 + fine / FINE)
    length = jnp.sqrt(squares / (AUG * AUG) + 1e-6)
    norm[...] = jnp.broadcast_to(length, (8, LANES))
    scale = jnp.minimum(1.0, CLIP / length) / AUG
    lane = lax.broadcasted_iota(jnp.int32, (SROWS, LANES), 1)
    for block in range(BLOCKS):
        value = None
        for a in range(LANES * block // COLS, (LANES * block + LANES - 1) // COLS + 1):
            begin = a * COLS - LANES * block
            piece = pltpu.roll(opened[a], begin % LANES, 1) * scale
            value = piece if value is None else jnp.where(lane >= begin, piece, value)
        lined[pl.ds(block, SROWS, stride=BLOCKS), :] = value
    lined[SROWS * BLOCKS:, :] = jnp.zeros((lined.shape[0] - SROWS * BLOCKS, LANES), jnp.float32)
    ahead = (index[0] * (SHARD % D)) % D
    rows = ahead // LANES
    lanes = ahead % LANES
    near = lined[pl.ds(rows, ROWS), :]
    far = lined[pl.ds(rows + 1, ROWS), :]
    lane = lax.broadcasted_iota(jnp.int32, (ROWS, LANES), 1)
    mixed = jnp.where(lane >= lanes, near, far)
    even[0:ROWS, :] = pltpu.roll(mixed, (LANES - lanes) % LANES, 1)
    even[ROWS:, :] = jnp.zeros((8, LANES), jnp.float32)
    place = lax.broadcasted_iota(jnp.int32, (8, LANES), 0) * LANES + lax.broadcasted_iota(jnp.int32, (8, LANES), 1)
    inside = place < SHARD - (ROWS - 8) * LANES
    even[ROWS - 8:ROWS, :] = jnp.where(inside, even[ROWS - 8:ROWS, :], 0.0)
    for j in range(term.shape[0]):
        term[j] = coded_chunk(even[PROWS * j:PROWS * j + 16, :])


def coded_chunk(block):
    row = lax.broadcasted_iota(jnp.int32, (16, LANES), 0)
    codes, level = encode(block, jnp.where(row < PROWS, jnp.abs(block), 0.0))
    return jnp.where(row < PROWS, codes, level).astype(jnp.int32).astype(jnp.int16)


def total_kernel(pieces, spread):
    total = jnp.zeros((16, LANES), jnp.float32)
    for i in range(pieces.shape[0]):
        piece = plain(pieces[i])
        total = total + piece * step_of(piece[PROWS:PROWS + 1])
    codes = coded_chunk(total)
    for j in range(spread.shape[0]):
        spread[j] = codes


def open_kernel(chunks, shard):
    for j in range(chunks.shape[0]):
        chunk = plain(chunks[j])
        value = chunk * step_of(chunk[PROWS:PROWS + 1])
        shard[PROWS * j:PROWS * (j + 1), :] = value[0:PROWS]


VMEM = pl.BlockSpec(memory_space=pltpu.VMEM)
SMEM = pl.BlockSpec(memory_space=pltpu.SMEM)


def per_device(images, offsets, flip_flags, out_grads, weight, gauss_noise):
    aug_index = lax.axis_index("aug")
    images_in_all = lax.axis_size("dp")
    blocks = out_grads[0, 0].T.reshape(AUG, COLS, GRID * GRID)
    blocks = lax.all_to_all(blocks, "aug", 0, 0, axis_index_groups=[ORDER])
    pat_early, pat_late = pl.pallas_call(
        patch_kernel,
        out_shape=(
            jax.ShapeDtypeStruct((PS, CH, 16, EARLY * SIDE), jnp.bfloat16),
            jax.ShapeDtypeStruct((2, PS, CH, 16, LATE * SIDE), jnp.bfloat16),
        ),
        in_specs=[SMEM, SMEM, VMEM],
        out_specs=(VMEM, VMEM),
        scratch_shapes=[
            pltpu.VMEM((SIDE, AUG * SIDE), jnp.bfloat16),
            pltpu.VMEM((CH, 2 * AUG, PITCH, LANES), jnp.float32),
        ],
        compiler_params=pltpu.CompilerParams(vmem_limit_bytes=20 * MIB),
        cost_estimate=pl.CostEstimate(
            flops=20_000_000_000, bytes_accessed=20_000_000, transcendentals=0
        ),
    )(offsets[0], flip_flags[0], images[0])
    parts = pl.pallas_call(
        gradient_kernel,
        out_shape=jax.ShapeDtypeStruct((AUG, MROWS, LANES), jnp.int16),
        in_specs=[VMEM, pl.BlockSpec(memory_space=pl.ANY), VMEM],
        out_specs=VMEM,
        scratch_shapes=[
            pltpu.VMEM((2, PS, CH, 16, LATE * SIDE), jnp.bfloat16),
            pltpu.VMEM((AUG * SIDE, COLS), jnp.bfloat16),
            pltpu.VMEM((PATCH + 12, LANES), jnp.float32),
            pltpu.VMEM((MROWS, LANES), jnp.float32),
            pltpu.VMEM((PS * CH * 16, LANES), jnp.float32),
            pltpu.SemaphoreType.DMA((2,)),
        ],
        compiler_params=pltpu.CompilerParams(vmem_limit_bytes=48 * MIB),
    )(pat_early, pat_late, blocks)
    parts = lax.all_to_all(parts, "aug", 0, 0, axis_index_groups=[ORDER])
    chunks = jax.ShapeDtypeStruct((images_in_all, 16, LANES), jnp.int16)
    term, norm = pl.pallas_call(
        shard_kernel,
        out_shape=(chunks, jax.ShapeDtypeStruct((8, LANES), jnp.float32)),
        in_specs=[SMEM, VMEM],
        out_specs=(VMEM, VMEM),
        scratch_shapes=[
            pltpu.VMEM((ROWS + 32, LANES), jnp.float32),
            pltpu.VMEM((ROWS + 8, LANES), jnp.float32),
        ],
        compiler_params=pltpu.CompilerParams(vmem_limit_bytes=8 * MIB),
    )(aug_index.reshape(1), parts)
    pieces = lax.all_to_all(term, "dp", 0, 0)
    spread = pl.pallas_call(
        total_kernel,
        out_shape=chunks,
        in_specs=[VMEM],
        out_specs=VMEM,
        compiler_params=pltpu.CompilerParams(vmem_limit_bytes=8 * MIB),
    )(pieces)
    gathered = lax.all_to_all(spread, "dp", 0, 0)
    shard = pl.pallas_call(
        open_kernel,
        out_shape=jax.ShapeDtypeStruct((ROWS, LANES), jnp.float32),
        in_specs=[VMEM],
        out_specs=VMEM,
        compiler_params=pltpu.CompilerParams(vmem_limit_bytes=8 * MIB),
    )(gathered)
    clipped_sum = shard.reshape(-1)[:SHARD]
    clipped_mean = clipped_sum / images_in_all
    new_weight = weight - 0.1 * (clipped_sum / CLIP + gauss_noise)
    return (new_weight, clipped_mean, norm[0, 0:1])


def solution(mesh):
    return jax.shard_map(
        per_device,
        mesh=mesh,
        in_specs=(
            P("dp", None, None, None),
            P("dp", None, None),
            P("dp", None),
            P("dp", "aug", None, None),
            P("aug"),
            P("aug"),
        ),
        out_specs=(P("aug"), P("aug"), P("dp")),
        check_vma=False,
    )
```
